128 devices in a mesh: dp: 16 (over x, y), proto: 8 (over z, core).
Axes of the slice: x: 4, y: 4, z: 4, core: 2. Of those that a mesh axis runs over, the one named last changes fastest.
Arguments:
- teacher_feat: bfloat16 [16384, 256], P('dp'), may hold values from -80 to 80
- student_feat: bfloat16 [16384, 256], P('dp'), may hold values from -80 to 80
- proto_weight: bfloat16 [256, 65536], P('dp', 'proto'), may hold values from -60 to 60
Outputs:
- weight_grad: float32 [256, 65536], P('dp', 'proto')
- loss: float32 [], replicated
The draws below stay inside these ranges and needn't reach their ends.
All inputs are finite; a program needn't handle non-finite values.
Results may differ from the reference program's by a relative error of at most 0.0004.
Values may be sent and summed in bfloat16 or wider, within the bound.
A program may use at most 192 MiB of HBM per device.

```python
import math
import jax
import jax.numpy as jnp
from jax import lax

D = 256
K = 65536
ITERS = 3
ROWS = 16384


cluster_count = 16


def heavy_entries(key, row_count, col_count, spread):
    entry_key, level_key = jax.random.split(key)
    entries = jnp.clip(jax.random.normal(entry_key, (row_count, col_count), jnp.float32), -4.0, 4.0)
    uniform_level = jax.random.uniform(level_key, (row_count, col_count), jnp.float32)
    return entries * jnp.exp(spread * uniform_level)


def cluster_directions(key):
    values = jax.random.normal(jax.random.fold_in(key, 101), (cluster_count, D), jnp.float32)
    return jnp.clip(values, -4.0, 4.0)


def cluster_signal(key):
    directions = cluster_directions(key)
    subkeys = jax.random.split(jax.random.fold_in(key, 103), 4)
    positions = jnp.arange(ROWS, dtype=jnp.int32)
    native = positions * cluster_count // ROWS
    strays = jax.random.randint(subkeys[0], (ROWS,), 0, 4) == 0
    others = jax.random.randint(subkeys[1], (ROWS,), 0, cluster_count)
    labels = jnp.where(strays, others, native)
    fraction = jnp.arange(cluster_count, dtype=jnp.float32) / (cluster_count - 1.0)
    levels = 2.0 + 6.0 * fraction * jax.random.uniform(subkeys[2], (cluster_count,), jnp.float32, 0.8, 1.2)
    row_gains = levels[labels] * jax.random.uniform(subkeys[3], (ROWS,), jnp.float32, 0.7, 1.3)
    return directions[labels] * row_gains[:, None]


def shared_view(key):
    return heavy_entries(key, ROWS, D, 2.5) + cluster_signal(key)


def draw_teacher_feat(key, part):
    shared = shared_view(key)
    key = jax.random.fold_in(key, 11)
    own_key = jax.random.fold_in(key, 0)
    values = shared + 0.5 * heavy_entries(own_key, ROWS, D, 2.5)
    return jnp.clip(values, -80.0, 80.0).astype(jnp.bfloat16)


def draw_student_feat(key, part):
    shared = shared_view(key)
    key = jax.random.fold_in(key, 23)
    own_key = jax.random.fold_in(key, 0)
    values = shared + 0.8 * heavy_entries(own_key, ROWS, D, 2.5)
    return jnp.clip(values, -80.0, 80.0).astype(jnp.bfloat16)


def draw_proto_weight(key, part):
    directions = cluster_directions(key)
    key = jax.random.fold_in(key, 37)
    noise_key, pick_key, again_key, align_key = jax.random.split(key, 4)
    labels = jnp.minimum(jax.random.randint(pick_key, (K,), 0, cluster_count), jax.random.randint(again_key, (K,), 0, cluster_count))
    alignment = jax.random.uniform(align_key, (K,), jnp.float32, 1.0, 8.0)
    signal = jnp.transpose(directions[labels]) * alignment[None, :]
    values = heavy_entries(noise_key, D, K, 2.5) + signal
    return jnp.clip(values, -60.0, 60.0).astype(jnp.bfloat16)


def setup_inputs(seed: int = 0) -> dict:
    splits = jax.random.split(jax.random.key(seed), 4)
    teacher_feat = draw_teacher_feat(jax.random.fold_in(splits[3], 71), 0)
    student_feat = draw_student_feat(jax.random.fold_in(splits[3], 71), 0)
    proto_weight = draw_proto_weight(jax.random.fold_in(splits[3], 71), 0)
    return {"teacher_feat": teacher_feat, "student_feat": student_feat, "proto_weight": proto_weight}


EPS = 1e-06
TEACHER_TEMP = 0.07
STUDENT_TEMP = 0.1

def unit_rows(feat):
    values = feat.astype(jnp.float32)
    scaled = values / jnp.sqrt(lax.optimization_barrier(jnp.sum(values * values, axis=1, keepdims=True)) + EPS)
    return scaled.astype(jnp.bfloat16)

def reference(teacher_feat, student_feat, proto_weight):
    t_hat = unit_rows(teacher_feat)
    s_hat = unit_rows(student_feat)
    weights = proto_weight.astype(jnp.float32)
    norms = jnp.sqrt(lax.optimization_barrier(jnp.sum(weights * weights, axis=0)) + EPS)
    block = math.gcd(ROWS, 512)
    nblocks = ROWS // block
    t_blocks = t_hat.reshape(nblocks, block, D)
    s_blocks = s_hat.reshape(nblocks, block, D)

    def cosine(rows):
        return jnp.dot(rows, proto_weight, preferred_element_type=jnp.float32) / norms

    def base(rows):
        return jnp.exp(cosine(rows) / TEACHER_TEMP)
    col_scale = jnp.ones((K,), jnp.float32)
    row_scale = jnp.ones((nblocks, block), jnp.float32)
    for step in range(ITERS):

        def add_cols(total, item):
            rows, scale = item
            return (total + lax.optimization_barrier(jnp.sum(base(rows) * scale[:, None], axis=0)), None)
        mass, unused = lax.scan(add_cols, jnp.zeros((K,), jnp.float32), (t_blocks, row_scale))
        col_scale = 1.0 / (mass * K)

        def row_mass(rows):
            return lax.optimization_barrier(jnp.sum(base(rows) * col_scale, axis=1))
        row_scale = 1.0 / (lax.map(row_mass, t_blocks) * ROWS)

    def finish(carry, item):
        loss_sum, grad_sum, col_sum = carry
        t_rows, s_rows, scale = item
        targets = base(t_rows) * col_scale * scale[:, None] * ROWS
        cos_s = cosine(s_rows)
        logits = cos_s / STUDENT_TEMP
        expo = jnp.exp(logits)
        total = lax.optimization_barrier(jnp.sum(expo, axis=1))
        lse = jnp.log(total)
        probs = expo / total[:, None]
        loss_sum = loss_sum + jnp.sum(targets * (lse[:, None] - logits))
        grad_cos = ((probs - targets) / (ROWS * STUDENT_TEMP)).astype(jnp.bfloat16)
        grad_sum = grad_sum + jnp.einsum('bd,bk->dk', s_rows.astype(jnp.float32), grad_cos.astype(jnp.float32))
        col_sum = col_sum + lax.optimization_barrier(jnp.sum(cos_s * grad_cos.astype(jnp.float32), axis=0))
        return ((loss_sum, grad_sum, col_sum), None)
    init = (jnp.zeros((), jnp.float32), jnp.zeros((D, K), jnp.float32), jnp.zeros((K,), jnp.float32))
    (loss_sum, grad_sum, col_sum), unused = lax.scan(finish, init, (t_blocks, s_blocks, row_scale))
    weight_grad = (grad_sum - weights / norms * col_sum) / norms
    return (weight_grad, loss_sum / ROWS)
```

```python
import functools
import math

import jax
import jax.numpy as jnp
from jax import lax
from jax.experimental import pallas as pl
from jax.experimental.pallas import tpu as pltpu
from jax.sharding import PartitionSpec as P

ITERS = 3
EPS = 1e-06
TEACHER_TEMP = 0.07
STUDENT_TEMP = 0.1
LOG2E = math.log2(math.e)
LANES = 128
MESH = pl.DeviceIdType.MESH
F32 = jnp.float32
BF16 = jnp.bfloat16

W_A2A, T_GATHER, S_GATHER = 0, 1, 2
COL = (3, 4, 5)
ROW = (6, 7, 8)
OUT_A2A, LOSS_PROTO, LOSS_DP = 9, 10, 11
W_PLUS, W_MINUS, W_HALF_A, W_HALF_B = 12, 13, 14, 15
W_CORE = 16
G_CORE = 20
G_HALF_A, G_HALF_B, G_PLUS, G_MINUS = 24, 25, 26, 27
STAGES = 28


def unit_rows(feat):
    values = feat.astype(F32)
    scaled = values / jnp.sqrt(jnp.sum(values * values, axis=1, keepdims=True) + EPS)
    return scaled.astype(BF16)


def fold_rows(x):
    n, c = x.shape
    return jnp.sum(x.reshape(n // 8, 8, c), axis=0)


def fold_lanes(x):
    total = x[:, :LANES]
    for j in range(1, x.shape[1] // LANES):
        total = total + x[:, j * LANES:(j + 1) * LANES]
    return total


def kernel(
    nd, np_, tile,
    teacher, student, weight,
    out, loss_out,
    t_raw, s_raw, t_all, s_all, s_t, w_all, e_ref,
    at_ref, as_ref, inv_ref, v_ref, rb_ref, sb_ref, racc, sacc,
    colx, rowx, g_tile, g_send, g_recv, g_own, half_a, half_b, g_z, out_recv,
    loss_p, loss_d,
    ssem, rsem, lsem,
):
    d = lax.axis_index("dp")
    p = lax.axis_index("proto")
    nz = np_ // 2
    partner = p + 1 - 2 * lax.rem(p, 2)
    plus = lax.rem(p + 2, np_)
    minus = lax.rem(p + np_ - 2, np_)
    chunk = t_raw.shape[0]
    rows = t_all.shape[0]
    depth, cols = w_all.shape[1:]
    own_depth = depth // nd
    ntiles = rows // tile
    total_rows = rows * np_
    total_cols = cols * np_ * nd

    def other(block):
        return block + 1 - 2 * lax.rem(block, 2)

    def remote(src, dst, stage, **where):
        return pltpu.make_async_remote_copy(
            src_ref=src, dst_ref=dst, send_sem=ssem.at[stage], recv_sem=rsem.at[stage],
            device_id=where, device_id_type=MESH)

    def to_all(axis, me, n, make):
        def step(o, carry):
            make(lax.rem(me + o, n), axis).start()
            return carry
        lax.fori_loop(1, n, step, 0)

    def wait_bytes(sem, ref):
        pltpu.make_async_copy(ref, ref, sem).wait()

    barrier = pltpu.get_barrier_semaphore()

    def greet(axis, me, n):
        def step(o, carry):
            pl.semaphore_signal(barrier, inc=1, device_id={axis: lax.rem(me + o, n)}, device_id_type=MESH)
            return carry
        lax.fori_loop(1, n, step, 0)

    greet("dp", d, nd)
    greet("proto", p, np_)

    load_t = pltpu.make_async_copy(teacher.at[pl.ds(p * chunk, chunk)], t_raw, lsem.at[0])
    load_s = pltpu.make_async_copy(student.at[pl.ds(p * chunk, chunk)], s_raw, lsem.at[1])
    own_rows = pl.ds(d * own_depth, own_depth)
    load_w = pltpu.make_async_copy(
        weight.at[:, pl.ds(d * cols, cols)], w_all.at[p, own_rows], lsem.at[2])
    load_t.start()
    load_s.start()
    load_w.start()
    load_t.wait()
    own_chunk = pl.ds(d * chunk, chunk)
    t_all[own_chunk, :] = unit_rows(t_raw[...])
    pl.semaphore_wait(barrier, nd + np_ - 2)

    to_all("dp", d, nd, lambda j, axis: remote(
        weight.at[:, pl.ds(j * cols, cols)], w_all.at[p, own_rows], W_A2A, **{axis: j}))
    to_all("dp", d, nd, lambda j, axis: remote(
        t_all.at[own_chunk], t_all.at[own_chunk], T_GATHER, **{axis: j}))
    load_s.wait()
    s_all[own_chunk, :] = unit_rows(s_raw[...])

    load_w.wait()
    wait_bytes(rsem.at[W_A2A], w_all.at[p, pl.ds(0, depth - own_depth)])
    half = depth // 2
    top, bottom = pl.ds(0, half), pl.ds(half, half)
    copies = []

    def go(copy):
        copy.start()
        copies.append(copy)
        return copy

    opposite = lax.rem(p + 4, np_)
    up = go(remote(w_all.at[p], w_all.at[p], W_PLUS, proto=plus))
    down = go(remote(w_all.at[p], w_all.at[p], W_MINUS, proto=minus))
    core = [None] * 4
    core[0] = go(remote(w_all.at[p], w_all.at[p], W_CORE, proto=partner))
    to_all("dp", d, nd, lambda j, axis: remote(
        s_all.at[own_chunk], s_all.at[own_chunk], S_GATHER, **{axis: j}))
    up.wait_recv()
    pass_a = go(remote(w_all.at[minus, top], w_all.at[minus, top], W_HALF_A, proto=plus))
    core[1] = go(remote(w_all.at[minus], w_all.at[minus], W_CORE + 1, proto=partner))
    down.wait_recv()
    pass_b = go(remote(w_all.at[plus, bottom], w_all.at[plus, bottom], W_HALF_B, proto=minus))
    core[2] = go(remote(w_all.at[plus], w_all.at[plus], W_CORE + 2, proto=partner))

    wait_bytes(rsem.at[T_GATHER], t_all.at[pl.ds(0, rows - chunk)])

    def first_pass(block):
        w = w_all[block].astype(F32)
        inv = 1.0 / jnp.sqrt(jnp.sum(w * w, axis=0, keepdims=True) + EPS)
        inv_ref[block] = inv
        at_ref[block] = inv * (LOG2E / TEACHER_TEMP)
        as_ref[block] = inv * (LOG2E / STUDENT_TEMP)

        def step(i, acc):
            part = pl.ds(i * tile, tile)
            dots = jnp.dot(t_all[part, :], w_all[block], preferred_element_type=F32)
            e = jnp.exp2(dots * at_ref[block])
            e_ref[block, part, :] = e
            return acc + fold_rows(e)

        acc = lax.fori_loop(0, ntiles, step, jnp.zeros((8, cols), F32))
        colx[0, p, block] = jnp.sum(acc, axis=0, keepdims=True)

    first_pass(p)
    core[0].wait_recv()
    first_pass(partner)
    first_pass(minus)
    first_pass(plus)
    core[1].wait_recv()
    first_pass(other(minus))
    core[2].wait_recv()
    first_pass(other(plus))
    pass_a.wait_recv()
    pass_b.wait_recv()
    core[3] = go(remote(w_all.at[opposite], w_all.at[opposite], W_CORE + 3, proto=partner))
    first_pass(opposite)
    core[3].wait_recv()
    first_pass(other(opposite))

    def send_cols(it):
        to_all("proto", p, np_, lambda j, axis: remote(
            colx.at[it, p], colx.at[it, p], COL[it], **{axis: j}))

    def take_cols(it):
        wait_bytes(rsem.at[COL[it]], colx.at[it, pl.ds(0, np_ - 1)])
        mass = colx[it, 0]
        for j in range(1, np_):
            mass = mass + colx[it, j]
        v_ref[...] = 1.0 / (mass * total_cols)

    def dense(acc_ref):
        lines = [
            jnp.sum(acc_ref[c * LANES:(c + 1) * LANES, :].T, axis=0, keepdims=True)
            for c in range(rows // LANES)]
        return jnp.concatenate(lines, axis=0)

    def spread(x, ref):
        for c in range(rows // LANES):
            ref[c * LANES:(c + 1) * LANES, :] = jnp.broadcast_to(x[c:c + 1, :], (LANES, LANES)).T

    def send_rows(it):
        def make(j, axis):
            if it < ITERS - 1:
                return remote(rowx.at[it, d, 0], rowx.at[it, d, 0], ROW[it], **{axis: j})
            return remote(rowx.at[it, d], rowx.at[it, d], ROW[it], **{axis: j})
        to_all("dp", d, nd, make)

    def row_total(it, kind):
        total = rowx[it, 0, kind]
        for j in range(1, nd):
            total = total + rowx[it, j, kind]
        return total

    def take_rows(it):
        if it < ITERS - 1:
            wait_bytes(rsem.at[ROW[it]], rowx.at[it, pl.ds(0, nd - 1), 0])
        else:
            wait_bytes(rsem.at[ROW[it]], rowx.at[it, pl.ds(0, nd - 1)])
        return 1.0 / (row_total(it, 0) * total_rows)

    lane_chunks = cols // LANES

    def row_pass(it):
        span = 64

        def step(i, carry):
            part = pl.ds(i * span, span)
            acc = None
            for b in range(np_):
                for j in range(lane_chunks):
                    lanes = slice(j * LANES, (j + 1) * LANES)
                    term = e_ref[b, part, lanes] * v_ref[b, :, lanes]
                    acc = term if acc is None else acc + term
            racc[part, :] = acc
            return carry

        lax.fori_loop(0, rows // span, step, 0)
        rowx[it, d, 0] = dense(racc)

    def col_pass(it):
        pair = 2

        def step(b2, carry):
            def inner(i, accs):
                accs = list(accs)
                for g in range(8):
                    part = pl.ds(i * 64 + g * 8, 8)
                    r = rb_ref[part, :]
                    for k in range(pair):
                        for j in range(lane_chunks):
                            n = k * lane_chunks + j
                            accs[n] = accs[n] + e_ref[b2 * pair + k, part, j * LANES:(j + 1) * LANES] * r
                return tuple(accs)

            zero = jnp.zeros((8, LANES), F32)
            accs = lax.fori_loop(0, rows // 64, inner, (zero,) * (pair * lane_chunks))
            for k in range(pair):
                for j in range(lane_chunks):
                    colx[it, p, b2 * pair + k, :, j * LANES:(j + 1) * LANES] = jnp.sum(
                        accs[k * lane_chunks + j], axis=0, keepdims=True)
            return carry

        lax.fori_loop(0, np_ // pair, step, 0)

    def student_pass(block, first):
        def step(i, carry):
            part = pl.ds(i * tile, tile)
            dots = jnp.dot(s_all[part, :], w_all[block], preferred_element_type=F32)
            sums = fold_lanes(jnp.exp2(dots * as_ref[block]))
            if first:
                sacc[part, :] = sums
            else:
                sacc[part, :] += sums
            return carry
        lax.fori_loop(0, ntiles, step, 0)

    send_cols(0)
    wait_bytes(rsem.at[S_GATHER], s_all.at[pl.ds(0, rows - chunk)])
    for c in range(rows // LANES):
        s_t[:, c * LANES:(c + 1) * LANES] = s_all[c * LANES:(c + 1) * LANES, :].T
    student_pass(0, True)
    student_pass(1, False)
    take_cols(0)
    row_pass(0)
    send_rows(0)
    student_pass(2, False)
    student_pass(3, False)
    spread(take_rows(0), rb_ref)
    col_pass(1)
    send_cols(1)
    student_pass(4, False)
    student_pass(5, False)
    take_cols(1)
    row_pass(1)
    send_rows(1)
    student_pass(6, False)
    student_pass(7, False)
    rowx[2, d, 1] = dense(sacc)
    spread(take_rows(1), rb_ref)
    col_pass(2)
    send_cols(2)
    take_cols(2)
    row_pass(2)
    send_rows(2)
    row_scale = take_rows(2)
    spread(row_scale * (1.0 / STUDENT_TEMP), rb_ref)
    soft_total = row_total(2, 1)
    spread(1.0 / (soft_total * (total_rows * STUDENT_TEMP)), sb_ref)
    lse = jnp.log(soft_total)

    def last_pass(block, dst, acc0):
        def step(i, acc):
            part = pl.ds(i * tile, tile)
            zb = jnp.dot(s_all[part, :], w_all[block], preferred_element_type=F32) * as_ref[block]
            es = jnp.exp2(zb)
            q_scale = rb_ref[part, :]
            p_scale = sb_ref[part, :]
            new = acc
            for j in range(lane_chunks):
                lanes = slice(j * LANES, (j + 1) * LANES)
                q = e_ref[block, part, lanes] * v_ref[block, :, lanes] * q_scale
                g_tile[part, lanes] = (es[:, lanes] * p_scale - q).astype(BF16)
                new = new + fold_rows(q * zb[:, lanes])
            return new

        acc = lax.fori_loop(0, ntiles, step, acc0)
        dst[...] = jnp.dot(s_t[...], g_tile[...], preferred_element_type=F32)
        return acc

    loss_acc = jnp.zeros((8, LANES), F32)
    owners = [opposite, plus, minus, p]
    gsends = [None] * 4
    left, right = slice(0, cols // 2), slice(cols // 2, cols)

    for n in range(4):
        own = owners[n]
        loss_acc = last_pass(other(own), g_send.at[n], loss_acc)
        gsends[n] = go(remote(g_send.at[n], g_recv.at[n], G_CORE + n, proto=partner))
        loss_acc = last_pass(own, g_own.at[n], loss_acc)
        gsends[n].wait_recv()
        if n == 0:
            g_own[0] += g_recv[0]
            ha = go(remote(g_own.at[0, top], half_a, G_HALF_A, proto=plus))
            hb = go(remote(g_own.at[0, bottom], half_b, G_HALF_B, proto=minus))
        elif n == 1:
            g_own[1, bottom] += g_recv[1, bottom]
            ha.wait_recv()
            g_own[1, top] = g_own[1, top] + g_recv[1, top] + half_a[...]
            gp = go(remote(g_own.at[1], g_z.at[0], G_PLUS, proto=plus))
        elif n == 2:
            g_own[2, top] += g_recv[2, top]
            hb.wait_recv()
            g_own[2, bottom] = g_own[2, bottom] + g_recv[2, bottom] + half_b[...]
            gm = go(remote(g_own.at[2], g_z.at[1], G_MINUS, proto=minus))

    first_line = lax.broadcasted_iota(jnp.int32, (8, LANES), 0) == 0
    lse_sum = jnp.broadcast_to(jnp.sum(lse, axis=0, keepdims=True) * (1.0 / nd), (8, LANES))
    loss_scale = total_rows * STUDENT_TEMP / LOG2E
    loss_p[p] = jnp.where(first_line, lse_sum, 0.0) - loss_acc * loss_scale
    to_all("proto", p, np_, lambda j, axis: remote(
        loss_p.at[p], loss_p.at[p], LOSS_PROTO, **{axis: j}))

    gp.wait_recv()
    gm.wait_recv()
    grad = g_own[3] + g_recv[3] + g_z[0] + g_z[1]
    inv = inv_ref[p]
    dirs = w_all[p].astype(F32) * inv
    col = jnp.sum(dirs * grad, axis=0, keepdims=True)
    g_own[3] = (grad - dirs * col) * inv
    to_all("dp", d, nd, lambda j, axis: remote(
        g_own.at[3, pl.ds(j * own_depth, own_depth)], out_recv.at[d], OUT_A2A, **{axis: j}))
    out_recv[d] = g_own[3, own_rows]

    wait_bytes(rsem.at[LOSS_PROTO], loss_p.at[pl.ds(0, np_ - 1)])
    part = loss_p[0]
    for j in range(1, np_):
        part = part + loss_p[j]
    loss_d[d] = part
    to_all("dp", d, nd, lambda j, axis: remote(
        loss_d.at[d], loss_d.at[d], LOSS_DP, **{axis: j}))
    wait_bytes(rsem.at[LOSS_DP], loss_d.at[pl.ds(0, nd - 1)])
    whole = loss_d[0]
    for j in range(1, nd):
        whole = whole + loss_d[j]
    loss_out[...] = jnp.broadcast_to(
        jnp.sum(jnp.sum(whole, axis=0, keepdims=True), axis=1, keepdims=True) * (1.0 / total_rows), (8, LANES))

    wait_bytes(rsem.at[OUT_A2A], out_recv.at[pl.ds(0, nd - 1)])
    for j in range(nd):
        out[:, j * cols:(j + 1) * cols] = out_recv[j]

    for copy in copies:
        copy.wait_send()
    wait_bytes(ssem.at[W_A2A], w_all.at[0, pl.ds(0, depth - own_depth)])
    wait_bytes(ssem.at[T_GATHER], t_all.at[pl.ds(0, rows - chunk)])
    wait_bytes(ssem.at[S_GATHER], s_all.at[pl.ds(0, rows - chunk)])
    for it in range(ITERS):
        wait_bytes(ssem.at[COL[it]], colx.at[it, pl.ds(0, np_ - 1)])
        if it < ITERS - 1:
            wait_bytes(ssem.at[ROW[it]], rowx.at[it, pl.ds(0, nd - 1), 0])
        else:
            wait_bytes(ssem.at[ROW[it]], rowx.at[it, pl.ds(0, nd - 1)])
    wait_bytes(ssem.at[OUT_A2A], out_recv.at[pl.ds(0, nd - 1)])
    wait_bytes(ssem.at[LOSS_PROTO], loss_p.at[pl.ds(0, np_ - 1)])
    wait_bytes(ssem.at[LOSS_DP], loss_d.at[pl.ds(0, nd - 1)])


def body(nd, np_, teacher_feat, student_feat, proto_weight):
    block_rows, depth = teacher_feat.shape
    own_depth, block_cols = proto_weight.shape
    chunk, cols = block_rows // np_, block_cols // nd
    rows = chunk * nd
    tile = min(256, rows)
    vmem = pltpu.VMEM
    out, loss = pl.pallas_call(
        functools.partial(kernel, nd, np_, tile),
        out_shape=(
            jax.ShapeDtypeStruct((own_depth, block_cols), F32),
            jax.ShapeDtypeStruct((8, LANES), F32),
        ),
        in_specs=[pl.BlockSpec(memory_space=pl.ANY)] * 3,
        out_specs=[pl.BlockSpec(memory_space=vmem)] * 2,
        scratch_shapes=[
            vmem((chunk, depth), BF16),
            vmem((chunk, depth), BF16),
            vmem((rows, depth), BF16),
            vmem((rows, depth), BF16),
            vmem((depth, rows), BF16),
            vmem((np_, depth, cols), BF16),
            vmem((np_, rows, cols), F32),
            vmem((np_, 1, cols), F32),
            vmem((np_, 1, cols), F32),
            vmem((np_, 1, cols), F32),
            vmem((np_, 1, cols), F32),
            vmem((rows, LANES), F32),
            vmem((rows, LANES), F32),
            vmem((rows, LANES), F32),
            vmem((rows, LANES), F32),
            vmem((ITERS, np_, np_, 1, cols), F32),
            vmem((ITERS, nd, 2, rows // LANES, LANES), F32),
            vmem((rows, cols), BF16),
            vmem((4, depth, cols), F32),
            vmem((4, depth, cols), F32),
            vmem((4, depth, cols), F32),
            vmem((depth // 2, cols), F32),
            vmem((depth // 2, cols), F32),
            vmem((2, depth, cols), F32),
            vmem((nd, own_depth, cols), F32),
            vmem((np_, 8, LANES), F32),
            vmem((nd, 8, LANES), F32),
            pltpu.SemaphoreType.DMA((STAGES,)),
            pltpu.SemaphoreType.DMA((STAGES,)),
            pltpu.SemaphoreType.DMA((3,)),
        ],
        compiler_params=pltpu.CompilerParams(
            collective_id=0, has_side_effects=True, vmem_limit_bytes=62 * 1024 * 1024),
        cost_estimate=pl.CostEstimate(
            flops=6 * rows * cols * np_ * depth, bytes_accessed=2 ** 21,
            transcendentals=2 * rows * cols * np_),
    )(teacher_feat, student_feat, proto_weight)
    return out, loss[0, 0]


def solution(mesh):
    nd, np_ = mesh.shape["dp"], mesh.shape["proto"]
    in_specs = (P("dp", None), P("dp", None), P("dp", "proto"))
    out_specs = (P("dp", "proto"), P())
    return jax.shard_map(
        functools.partial(body, nd, np_), mesh=mesh, in_specs=in_specs, out_specs=out_specs, check_vma=False)
```

```python
import functools
import math

import jax
import jax.numpy as jnp
from jax import lax
from jax.experimental import pallas as pl
from jax.experimental.pallas import tpu as pltpu
from jax.sharding import PartitionSpec as P

ITERS = 3
EPS = 1e-06
TEACHER_TEMP = 0.07
STUDENT_TEMP = 0.1
LOG2E = math.log2(math.e)
LANES = 128
MESH = pl.DeviceIdType.MESH
F32 = jnp.float32
BF16 = jnp.bfloat16

W_A2A, T_GATHER, S_GATHER = 0, 1, 2
COL = (3, 4, 5)
ROW = (6, 7, 8)
LOSS_PROTO, LOSS_DP = 10, 11
W_PLUS, W_MINUS, W_HALF_A, W_HALF_B = 12, 13, 14, 15
W_CORE = 16
G_CORE = 20
G_HALF_A, G_HALF_B = 28, 29
G_PLUS, G_MINUS = 30, 32
OUT_A2A = 34
STAGES = 36


def unit_rows(feat):
    values = feat.astype(F32)
    scaled = values / jnp.sqrt(jnp.sum(values * values, axis=1, keepdims=True) + EPS)
    return scaled.astype(BF16)


def fold_rows(x):
    n, c = x.shape
    return jnp.sum(x.reshape(n // 8, 8, c), axis=0)


def fold_lanes(x):
    total = x[:, :LANES]
    for j in range(1, x.shape[1] // LANES):
        total = total + x[:, j * LANES:(j + 1) * LANES]
    return total


def kernel(
    nd, np_, tile,
    teacher, student, weight,
    out, loss_out,
    t_raw, s_raw, t_all, s_all, s_t, w_all, e_ref,
    at_ref, as_ref, inv_ref, v_ref, rb_ref, sb_ref, racc, sacc,
    colx, rowx, g_tiles, g_send, g_recv, g_own, half_a, half_b, g_z, out_recv,
    loss_p, loss_d,
    ssem, rsem, lsem,
):
    d = lax.axis_index("dp")
    p = lax.axis_index("proto")
    nz = np_ // 2
    partner = p + 1 - 2 * lax.rem(p, 2)
    plus = lax.rem(p + 2, np_)
    minus = lax.rem(p + np_ - 2, np_)
    chunk = t_raw.shape[0]
    rows = t_all.shape[0]
    depth, cols = w_all.shape[1:]
    own_depth = depth // nd
    ntiles = rows // tile
    total_rows = rows * np_
    total_cols = cols * np_ * nd

    def other(block):
        return block + 1 - 2 * lax.rem(block, 2)

    def remote(src, dst, stage, **where):
        return pltpu.make_async_remote_copy(
            src_ref=src, dst_ref=dst, send_sem=ssem.at[stage], recv_sem=rsem.at[stage],
            device_id=where, device_id_type=MESH)

    def to_all(axis, me, n, make):
        def step(o, carry):
            make(lax.rem(me + o, n), axis).start()
            return carry
        lax.fori_loop(1, n, step, 0)

    def wait_bytes(sem, ref):
        pltpu.make_async_copy(ref, ref, sem).wait()

    barrier = pltpu.get_barrier_semaphore()

    def greet(axis, me, n):
        def step(o, carry):
            pl.semaphore_signal(barrier, inc=1, device_id={axis: lax.rem(me + o, n)}, device_id_type=MESH)
            return carry
        lax.fori_loop(1, n, step, 0)

    greet("dp", d, nd)
    greet("proto", p, np_)

    load_t = pltpu.make_async_copy(teacher.at[pl.ds(p * chunk, chunk)], t_raw, lsem.at[0])
    load_s = pltpu.make_async_copy(student.at[pl.ds(p * chunk, chunk)], s_raw, lsem.at[1])
    own_rows = pl.ds(d * own_depth, own_depth)
    load_w = pltpu.make_async_copy(
        weight.at[:, pl.ds(d * cols, cols)], w_all.at[p, own_rows], lsem.at[2])
    load_t.start()
    load_s.start()
    load_w.start()
    load_t.wait()
    own_chunk = pl.ds(d * chunk, chunk)
    t_all[own_chunk, :] = unit_rows(t_raw[...])
    pl.semaphore_wait(barrier, nd + np_ - 2)

    to_all("dp", d, nd, lambda j, axis: remote(
        weight.at[:, pl.ds(j * cols, cols)], w_all.at[p, own_rows], W_A2A, **{axis: j}))
    load_s.wait()
    s_all[own_chunk, :] = unit_rows(s_raw[...])

    load_w.wait()
    wait_bytes(rsem.at[W_A2A], w_all.at[p, pl.ds(0, depth - own_depth)])
    half = depth // 2
    top, bottom = pl.ds(0, half), pl.ds(half, half)
    copies = []

    def go(copy):
        copy.start()
        copies.append(copy)
        return copy

    opposite = lax.rem(p + 4, np_)
    up = go(remote(w_all.at[p], w_all.at[p], W_PLUS, proto=plus))
    down = go(remote(w_all.at[p], w_all.at[p], W_MINUS, proto=minus))
    core = [None] * 4
    core[0] = go(remote(w_all.at[p], w_all.at[p], W_CORE, proto=partner))
    to_all("dp", d, nd, lambda j, axis: remote(
        t_all.at[own_chunk], t_all.at[own_chunk], T_GATHER, **{axis: j}))
    up.wait_recv()
    pass_a = go(remote(w_all.at[minus, top], w_all.at[minus, top], W_HALF_A, proto=plus))
    core[1] = go(remote(w_all.at[minus], w_all.at[minus], W_CORE + 1, proto=partner))
    down.wait_recv()
    pass_b = go(remote(w_all.at[plus, bottom], w_all.at[plus, bottom], W_HALF_B, proto=minus))
    core[2] = go(remote(w_all.at[plus], w_all.at[plus], W_CORE + 2, proto=partner))

    wait_bytes(rsem.at[T_GATHER], t_all.at[pl.ds(0, rows - chunk)])
    to_all("dp", d, nd, lambda j, axis: remote(
        s_all.at[own_chunk], s_all.at[own_chunk], S_GATHER, **{axis: j}))

    def first_pass(block):
        w = w_all[block].astype(F32)
        inv = 1.0 / jnp.sqrt(jnp.sum(w * w, axis=0, keepdims=True) + EPS)
        inv_ref[block] = inv
        at_ref[block] = inv * (LOG2E / TEACHER_TEMP)
        as_ref[block] = inv * (LOG2E / STUDENT_TEMP)

        acc = jnp.zeros((8, cols), F32)
        for i in range(ntiles):
            part = slice(i * tile, (i + 1) * tile)
            dots = jnp.dot(t_all[part, :], w_all[block], preferred_element_type=F32)
            e = jnp.exp2(dots * at_ref[block])
            e_ref[block, part, :] = e
            acc = acc + fold_rows(e)
        colx[0, p, block] = jnp.sum(acc, axis=0, keepdims=True)

    first_pass(p)
    core[0].wait_recv()
    first_pass(partner)
    first_pass(minus)
    first_pass(plus)
    core[1].wait_recv()
    first_pass(other(minus))
    core[2].wait_recv()
    first_pass(other(plus))
    pass_a.wait_recv()
    pass_b.wait_recv()
    core[3] = go(remote(w_all.at[opposite], w_all.at[opposite], W_CORE + 3, proto=partner))
    first_pass(opposite)
    core[3].wait_recv()
    first_pass(other(opposite))

    def send_cols(it):
        to_all("proto", p, np_, lambda j, axis: remote(
            colx.at[it, p], colx.at[it, p], COL[it], **{axis: j}))

    def take_cols(it):
        wait_bytes(rsem.at[COL[it]], colx.at[it, pl.ds(0, np_ - 1)])
        mass = colx[it, 0]
        for j in range(1, np_):
            mass = mass + colx[it, j]
        v_ref[...] = 1.0 / (mass * total_cols)

    def dense(acc_ref):
        lines = [
            jnp.sum(acc_ref[c * LANES:(c + 1) * LANES, :].T, axis=0, keepdims=True)
            for c in range(rows // LANES)]
        return jnp.concatenate(lines, axis=0)

    def spread(x, ref):
        for c in range(rows // LANES):
            ref[c * LANES:(c + 1) * LANES, :] = jnp.broadcast_to(x[c:c + 1, :], (LANES, LANES)).T

    def send_rows(it):
        def make(j, axis):
            if it < ITERS - 1:
                return remote(rowx.at[it, d, 0], rowx.at[it, d, 0], ROW[it], **{axis: j})
            return remote(rowx.at[it, d], rowx.at[it, d], ROW[it], **{axis: j})
        to_all("dp", d, nd, make)

    def row_total(it, kind):
        total = rowx[it, 0, kind]
        for j in range(1, nd):
            total = total + rowx[it, j, kind]
        return total

    def take_rows(it):
        if it < ITERS - 1:
            wait_bytes(rsem.at[ROW[it]], rowx.at[it, pl.ds(0, nd - 1), 0])
        else:
            wait_bytes(rsem.at[ROW[it]], rowx.at[it, pl.ds(0, nd - 1)])
        return 1.0 / (row_total(it, 0) * total_rows)

    lane_chunks = cols // LANES

    def row_pass(it):
        span = 64

        def step(i, carry):
            part = pl.ds(i * span, span)
            acc = None
            for b in range(np_):
                for j in range(lane_chunks):
                    lanes = slice(j * LANES, (j + 1) * LANES)
                    term = e_ref[b, part, lanes] * v_ref[b, :, lanes]
                    acc = term if acc is None else acc + term
            racc[part, :] = acc
            return carry

        lax.fori_loop(0, rows // span, step, 0)
        rowx[it, d, 0] = dense(racc)

    def col_pass(it):
        pair = 2

        def step(b2, carry):
            def inner(i, accs):
                accs = list(accs)
                for g in range(8):
                    part = pl.ds(i * 64 + g * 8, 8)
                    r = rb_ref[part, :]
                    for k in range(pair):
                        for j in range(lane_chunks):
                            n = k * lane_chunks + j
                            accs[n] = accs[n] + e_ref[b2 * pair + k, part, j * LANES:(j + 1) * LANES] * r
                return tuple(accs)

            zero = jnp.zeros((8, LANES), F32)
            accs = lax.fori_loop(0, rows // 64, inner, (zero,) * (pair * lane_chunks))
            for k in range(pair):
                for j in range(lane_chunks):
                    colx[it, p, b2 * pair + k, :, j * LANES:(j + 1) * LANES] = jnp.sum(
                        accs[k * lane_chunks + j], axis=0, keepdims=True)
            return carry

        lax.fori_loop(0, np_ // pair, step, 0)

    def student_pass(first, last):
        def step(block, carry):
            for i in range(ntiles):
                part = slice(i * tile, (i + 1) * tile)
                dots = jnp.dot(s_all[part, :], w_all[block], preferred_element_type=F32)
                sums = fold_lanes(jnp.exp2(dots * as_ref[block]))
                sacc[part, :] += sums
            return carry
        lax.fori_loop(first, last, step, 0)

    send_cols(0)
    wait_bytes(rsem.at[S_GATHER], s_all.at[pl.ds(0, rows - chunk)])
    for c in range(rows // LANES):
        s_t[:, c * LANES:(c + 1) * LANES] = s_all[c * LANES:(c + 1) * LANES, :].T
    sacc[...] = jnp.zeros_like(sacc)
    student_pass(0, 2)
    take_cols(0)
    row_pass(0)
    send_rows(0)
    student_pass(2, 4)
    spread(take_rows(0), rb_ref)
    col_pass(1)
    send_cols(1)
    student_pass(4, 6)
    take_cols(1)
    row_pass(1)
    send_rows(1)
    student_pass(6, 8)
    rowx[2, d, 1] = dense(sacc)
    spread(take_rows(1), rb_ref)
    col_pass(2)
    send_cols(2)
    take_cols(2)
    row_pass(2)
    send_rows(2)
    row_scale = take_rows(2)
    spread(row_scale * (1.0 / STUDENT_TEMP), rb_ref)
    soft_total = row_total(2, 1)
    spread(1.0 / (soft_total * (total_rows * STUDENT_TEMP)), sb_ref)
    lse = jnp.log(soft_total)

    half_cols = cols // 2

    def unit(block, side, g_tile, acc):
        base = side * half_cols
        columns = slice(base, base + half_cols)
        for i in range(ntiles):
            part = slice(i * tile, (i + 1) * tile)
            zb = jnp.dot(s_all[part, :], w_all[block, :, columns],
                         preferred_element_type=F32) * as_ref[block, :, columns]
            es = jnp.exp2(zb)
            q_scale = rb_ref[part, :]
            p_scale = sb_ref[part, :]
            for j in range(half_cols // LANES):
                lanes = slice(j * LANES, (j + 1) * LANES)
                here = slice(base + j * LANES, base + (j + 1) * LANES)
                q = e_ref[block, part, here] * v_ref[block, :, here] * q_scale
                g_tile[part, lanes] = (es[:, lanes] * p_scale - q).astype(BF16)
                acc = acc + fold_rows(q * zb[:, lanes])
        return acc

    owners = [opposite, plus, minus, p]
    z_copies = {}
    core_copies = {}

    def chip_sum(n, side):
        core_copies[n, side].wait_recv()
        if (n, side) == (1, 0):
            z_copies["a"].wait_recv()
            g_own[n, side] = g_own[n, side] + g_recv[n, side] + half_a[...]
        elif (n, side) == (2, 1):
            z_copies["b"].wait_recv()
            g_own[n, side] = g_own[n, side] + g_recv[n, side] + half_b[...]
        else:
            g_own[n, side] += g_recv[n, side]
        mine = g_own.at[n, side]
        if (n, side) == (0, 0):
            z_copies["a"] = go(remote(mine, half_a, G_HALF_A, proto=plus))
        elif (n, side) == (0, 1):
            z_copies["b"] = go(remote(mine, half_b, G_HALF_B, proto=minus))
        elif n == 1:
            z_copies[0, side] = go(remote(mine, g_z.at[0, side], G_PLUS + side, proto=plus))
        elif n == 2:
            z_copies[1, side] = go(remote(mine, g_z.at[1, side], G_MINUS + side, proto=minus))

    def gradient(n, side, is_own, g_tile):
        dst = g_own if is_own else g_send
        dst[n, side] = jnp.dot(s_t[...], g_tile[...], preferred_element_type=F32)

    order = [(0, 0), (0, 1), (1, 1), (2, 0), (3, 0), (3, 1), (1, 0), (2, 1)]
    units = [(n, side, is_own) for n, side in order for is_own in (False, True)]
    loss_acc = jnp.zeros((8, LANES), F32)
    waiting = None
    for k in range(len(units) + 2):
        if 0 < k <= len(units):
            gradient(*units[k - 1], g_tiles.at[(k - 1) % 2])
        if k < len(units):
            n, side, is_own = units[k]
            block = owners[n] if is_own else other(owners[n])
            loss_acc = unit(block, side, g_tiles.at[k % 2], loss_acc)
        if waiting is not None:
            chip_sum(*waiting)
            waiting = None
        if 0 < k <= len(units):
            n, side, is_own = units[k - 1]
            if is_own:
                waiting = (n, side)
            else:
                core_copies[n, side] = go(remote(
                    g_send.at[n, side], g_recv.at[n, side], G_CORE + 2 * n + side, proto=partner))

    first_line = lax.broadcasted_iota(jnp.int32, (8, LANES), 0) == 0
    lse_sum = jnp.broadcast_to(jnp.sum(lse, axis=0, keepdims=True) * (1.0 / nd), (8, LANES))
    loss_scale = total_rows * STUDENT_TEMP / LOG2E
    loss_p[p] = jnp.where(first_line, lse_sum, 0.0) - loss_acc * loss_scale
    to_all("proto", p, np_, lambda j, axis: remote(
        loss_p.at[p], loss_p.at[p], LOSS_PROTO, **{axis: j}))
    wait_bytes(rsem.at[LOSS_PROTO], loss_p.at[pl.ds(0, np_ - 1)])
    part = loss_p[0]
    for j in range(1, np_):
        part = part + loss_p[j]
    loss_d[d] = part
    to_all("dp", d, nd, lambda j, axis: remote(
        loss_d.at[d], loss_d.at[d], LOSS_DP, **{axis: j}))

    for side in (0, 1):
        columns = slice(side * half_cols, (side + 1) * half_cols)
        z_copies[0, side].wait_recv()
        z_copies[1, side].wait_recv()
        grad = g_own[3, side] + g_z[0, side] + g_z[1, side]
        inv = inv_ref[p, :, columns]
        dirs = w_all[p, :, columns].astype(F32) * inv
        col = jnp.sum(dirs * grad, axis=0, keepdims=True)
        g_own[3, side] = (grad - dirs * col) * inv
        to_all("dp", d, nd, lambda j, axis: remote(
            g_own.at[3, side, pl.ds(j * own_depth, own_depth)], out_recv.at[side, d],
            OUT_A2A + side, **{axis: j}))
        out_recv[side, d] = g_own[3, side, own_rows]

    wait_bytes(rsem.at[LOSS_DP], loss_d.at[pl.ds(0, nd - 1)])
    whole = loss_d[0]
    for j in range(1, nd):
        whole = whole + loss_d[j]
    loss_out[...] = jnp.broadcast_to(
        jnp.sum(jnp.sum(whole, axis=0, keepdims=True), axis=1, keepdims=True) * (1.0 / total_rows), (8, LANES))

    for side in (0, 1):
        wait_bytes(rsem.at[OUT_A2A + side], out_recv.at[side, pl.ds(0, nd - 1)])
        for j in range(nd):
            base = j * cols + side * half_cols
            out[:, base:base + half_cols] = out_recv[side, j]

    for copy in copies:
        copy.wait_send()
    wait_bytes(ssem.at[W_A2A], w_all.at[0, pl.ds(0, depth - own_depth)])
    wait_bytes(ssem.at[T_GATHER], t_all.at[pl.ds(0, rows - chunk)])
    wait_bytes(ssem.at[S_GATHER], s_all.at[pl.ds(0, rows - chunk)])
    for it in range(ITERS):
        wait_bytes(ssem.at[COL[it]], colx.at[it, pl.ds(0, np_ - 1)])
        if it < ITERS - 1:
            wait_bytes(ssem.at[ROW[it]], rowx.at[it, pl.ds(0, nd - 1), 0])
        else:
            wait_bytes(ssem.at[ROW[it]], rowx.at[it, pl.ds(0, nd - 1)])
    for side in (0, 1):
        wait_bytes(ssem.at[OUT_A2A + side], out_recv.at[side, pl.ds(0, nd - 1)])
    wait_bytes(ssem.at[LOSS_PROTO], loss_p.at[pl.ds(0, np_ - 1)])
    wait_bytes(ssem.at[LOSS_DP], loss_d.at[pl.ds(0, nd - 1)])


def body(nd, np_, teacher_feat, student_feat, proto_weight):
    block_rows, depth = teacher_feat.shape
    own_depth, block_cols = proto_weight.shape
    chunk, cols = block_rows // np_, block_cols // nd
    rows = chunk * nd
    tile = min(256, rows)
    vmem = pltpu.VMEM
    out, loss = pl.pallas_call(
        functools.partial(kernel, nd, np_, tile),
        out_shape=(
            jax.ShapeDtypeStruct((own_depth, block_cols), F32),
            jax.ShapeDtypeStruct((8, LANES), F32),
        ),
        in_specs=[pl.BlockSpec(memory_space=pl.ANY)] * 3,
        out_specs=[pl.BlockSpec(memory_space=vmem)] * 2,
        scratch_shapes=[
            vmem((chunk, depth), BF16),
            vmem((chunk, depth), BF16),
            vmem((rows, depth), BF16),
            vmem((rows, depth), BF16),
            vmem((depth, rows), BF16),
            vmem((np_, depth, cols), BF16),
            vmem((np_, rows, cols), F32),
            vmem((np_, 1, cols), F32),
            vmem((np_, 1, cols), F32),
            vmem((np_, 1, cols), F32),
            vmem((np_, 1, cols), F32),
            vmem((rows, LANES), F32),
            vmem((rows, LANES), F32),
            vmem((rows, LANES), F32),
            vmem((rows, LANES), F32),
            vmem((ITERS, np_, np_, 1, cols), F32),
            vmem((ITERS, nd, 2, rows // LANES, LANES), F32),
            vmem((2, rows, cols // 2), BF16),
            vmem((4, 2, depth, cols // 2), F32),
            vmem((4, 2, depth, cols // 2), F32),
            vmem((4, 2, depth, cols // 2), F32),
            vmem((depth, cols // 2), F32),
            vmem((depth, cols // 2), F32),
            vmem((2, 2, depth, cols // 2), F32),
            vmem((2, nd, own_depth, cols // 2), F32),
            vmem((np_, 8, LANES), F32),
            vmem((nd, 8, LANES), F32),
            pltpu.SemaphoreType.DMA((STAGES,)),
            pltpu.SemaphoreType.DMA((STAGES,)),
            pltpu.SemaphoreType.DMA((3,)),
        ],
        compiler_params=pltpu.CompilerParams(
            collective_id=0, has_side_effects=True, vmem_limit_bytes=62 * 1024 * 1024),
        cost_estimate=pl.CostEstimate(
            flops=6 * rows * cols * np_ * depth, bytes_accessed=2 ** 21,
            transcendentals=2 * rows * cols * np_),
    )(teacher_feat, student_feat, proto_weight)
    return out, loss[0, 0]


def solution(mesh):
    nd, np_ = mesh.shape["dp"], mesh.shape["proto"]
    in_specs = (P("dp", None), P("dp", None), P("dp", "proto"))
    out_specs = (P("dp", "proto"), P())
    return jax.shard_map(
        functools.partial(body, nd, np_), mesh=mesh, in_specs=in_specs, out_specs=out_specs, check_vma=False)
```

```python
import functools
import math

import jax
import jax.numpy as jnp
from jax import lax
from jax.experimental import pallas as pl
from jax.experimental.pallas import tpu as pltpu
from jax.sharding import PartitionSpec as P

ITERS = 3
EPS = 1e-06
TEACHER_TEMP = 0.07
STUDENT_TEMP = 0.1
LOG2E = math.log2(math.e)
LANES = 128
MESH = pl.DeviceIdType.MESH
F32 = jnp.float32
BF16 = jnp.bfloat16

W_A2A, T_GATHER, S_GATHER = 0, 1, 2
SOFT = 3
LOSS_PROTO, LOSS_DP = 4, 5
W_PLUS, W_MINUS = 6, 8
W_HALF_A, W_HALF_B = 10, 11
W_CORE = 16
G_CORE = 20
G_HALF_A, G_HALF_B = 28, 29
G_PLUS, G_MINUS = 30, 32
OUT_A2A = 34
COL = 36
ROW = 42
STAGES = 48


def unit_rows(feat):
    values = feat.astype(F32)
    scaled = values / jnp.sqrt(jnp.sum(values * values, axis=1, keepdims=True) + EPS)
    return scaled.astype(BF16)


def fold_rows(x):
    n, c = x.shape
    return jnp.sum(x.reshape(n // 8, 8, c), axis=0)


def fold_lanes(x):
    total = x[:, :LANES]
    for j in range(1, x.shape[1] // LANES):
        total = total + x[:, j * LANES:(j + 1) * LANES]
    return total


def kernel(
    nd, np_, tile,
    teacher, student, weight,
    out, loss_out,
    t_raw, s_raw, t_all, s_all, s_t, w_all, e_ref,
    at_ref, as_ref, inv_ref, v_ref, rb_ref, sb_ref, racc, sacc,
    cacc, colx, rowx, soft, g_tiles, g_send, g_recv, g_own, half_a, half_b, g_z, out_recv,
    loss_p, loss_d,
    ssem, rsem, lsem,
):
    d = lax.axis_index("dp")
    p = lax.axis_index("proto")
    nz = np_ // 2
    partner = p + 1 - 2 * lax.rem(p, 2)
    plus = lax.rem(p + 2, np_)
    minus = lax.rem(p + np_ - 2, np_)
    chunk = t_raw.shape[0]
    rows = t_all.shape[0]
    depth, cols = w_all.shape[1:]
    own_depth = depth // nd
    ntiles = rows // tile
    total_rows = rows * np_
    total_cols = cols * np_ * nd

    def other(block):
        return block + 1 - 2 * lax.rem(block, 2)

    def remote(src, dst, stage, **where):
        return pltpu.make_async_remote_copy(
            src_ref=src, dst_ref=dst, send_sem=ssem.at[stage], recv_sem=rsem.at[stage],
            device_id=where, device_id_type=MESH)

    def to_all(axis, me, n, make):
        def step(o, carry):
            make(lax.rem(me + o, n), axis).start()
            return carry
        lax.fori_loop(1, n, step, 0)

    def wait_bytes(sem, ref):
        pltpu.make_async_copy(ref, ref, sem).wait()

    barrier = pltpu.get_barrier_semaphore()

    def greet(axis, me, n):
        def step(o, carry):
            pl.semaphore_signal(barrier, inc=1, device_id={axis: lax.rem(me + o, n)}, device_id_type=MESH)
            return carry
        lax.fori_loop(1, n, step, 0)

    greet("dp", d, nd)
    greet("proto", p, np_)

    load_t = pltpu.make_async_copy(teacher.at[pl.ds(p * chunk, chunk)], t_raw, lsem.at[0])
    load_s = pltpu.make_async_copy(student.at[pl.ds(p * chunk, chunk)], s_raw, lsem.at[1])
    own_rows = pl.ds(d * own_depth, own_depth)
    load_w = pltpu.make_async_copy(
        weight.at[:, pl.ds(d * cols, cols)], w_all.at[p, own_rows], lsem.at[2])
    load_t.start()
    load_s.start()
    load_w.start()
    load_t.wait()
    own_chunk = pl.ds(d * chunk, chunk)
    t_all[own_chunk, :] = unit_rows(t_raw[...])
    pl.semaphore_wait(barrier, nd + np_ - 2)

    to_all("dp", d, nd, lambda j, axis: remote(
        weight.at[:, pl.ds(j * cols, cols)], w_all.at[p, own_rows], W_A2A, **{axis: j}))
    load_s.wait()
    s_all[own_chunk, :] = unit_rows(s_raw[...])

    load_w.wait()
    wait_bytes(rsem.at[W_A2A], w_all.at[p, pl.ds(0, depth - own_depth)])
    half = depth // 2
    top, bottom = pl.ds(0, half), pl.ds(half, half)
    copies = []

    def go(copy):
        copy.start()
        copies.append(copy)
        return copy

    opposite = lax.rem(p + 4, np_)
    def ring(part, stage, to):
        return remote(w_all.at[p, part], w_all.at[p, part], stage, proto=to)

    up_top = go(ring(top, W_PLUS, plus))
    down_bottom = go(ring(bottom, W_MINUS, minus))
    core = [None] * 4
    core[0] = go(remote(w_all.at[p], w_all.at[p], W_CORE, proto=partner))
    to_all("dp", d, nd, lambda j, axis: remote(
        t_all.at[own_chunk], t_all.at[own_chunk], T_GATHER, **{axis: j}))
    up_top.wait_send()
    up_bottom = go(ring(bottom, W_PLUS + 1, plus))
    down_bottom.wait_send()
    down_top = go(ring(top, W_MINUS + 1, minus))
    up_top.wait_recv()
    pass_a = go(remote(w_all.at[minus, top], w_all.at[minus, top], W_HALF_A, proto=plus))
    down_bottom.wait_recv()
    pass_b = go(remote(w_all.at[plus, bottom], w_all.at[plus, bottom], W_HALF_B, proto=minus))
    up_bottom.wait_recv()
    core[1] = go(remote(w_all.at[minus], w_all.at[minus], W_CORE + 1, proto=partner))
    down_top.wait_recv()
    core[2] = go(remote(w_all.at[plus], w_all.at[plus], W_CORE + 2, proto=partner))

    wait_bytes(rsem.at[T_GATHER], t_all.at[pl.ds(0, rows - chunk)])
    to_all("dp", d, nd, lambda j, axis: remote(
        s_all.at[own_chunk], s_all.at[own_chunk], S_GATHER, **{axis: j}))

    def first_pass(block):
        w = w_all[block].astype(F32)
        inv = 1.0 / jnp.sqrt(jnp.sum(w * w, axis=0, keepdims=True) + EPS)
        inv_ref[block] = inv
        at_ref[block] = inv * (LOG2E / TEACHER_TEMP)
        as_ref[block] = inv * (LOG2E / STUDENT_TEMP)

        acc = jnp.zeros((8, cols), F32)
        for i in range(ntiles):
            part = slice(i * tile, (i + 1) * tile)
            dots = jnp.dot(t_all[part, :], w_all[block], preferred_element_type=F32)
            e = jnp.exp2(dots * at_ref[block])
            e_ref[block, part, :] = e
            acc = acc + fold_rows(e)
        colx[0, p, block] = jnp.sum(acc, axis=0, keepdims=True)

    first_pass(p)
    core[0].wait_recv()
    first_pass(partner)
    first_pass(minus)
    first_pass(plus)
    core[1].wait_recv()
    first_pass(other(minus))
    core[2].wait_recv()
    first_pass(other(plus))
    pass_a.wait_recv()
    pass_b.wait_recv()
    core[3] = go(remote(w_all.at[opposite], w_all.at[opposite], W_CORE + 3, proto=partner))
    first_pass(opposite)
    core[3].wait_recv()
    first_pass(other(opposite))

    half_blocks, half_rows = np_ // 2, rows // 2
    lines = rows // LANES
    half_lines = lines // 2
    lane_chunks = cols // LANES

    def some_blocks(h):
        return pl.ds(h * half_blocks, half_blocks)

    def some_lines(h):
        return pl.ds(h * half_lines, half_lines)

    def send_cols(it, h):
        mine = colx.at[it, p, some_blocks(h)]
        to_all("proto", p, np_, lambda j, axis: remote(mine, mine, COL + 2 * it + h, **{axis: j}))

    def take_cols(it, h):
        wait_bytes(rsem.at[COL + 2 * it + h], colx.at[it, pl.ds(0, np_ - 1), some_blocks(h)])
        mass = colx[it, 0, some_blocks(h)]
        for j in range(1, np_):
            mass = mass + colx[it, j, some_blocks(h)]
        v_ref[some_blocks(h)] = 1.0 / (mass * total_cols)

    def dense(acc_ref, first, last):
        sums = [
            jnp.sum(acc_ref[c * LANES:(c + 1) * LANES, :].T, axis=0, keepdims=True)
            for c in range(first, last)]
        return jnp.concatenate(sums, axis=0)

    def spread(x, ref, first):
        for c in range(x.shape[0]):
            at = (first + c) * LANES
            ref[at:at + LANES, :] = jnp.broadcast_to(x[c:c + 1, :], (LANES, LANES)).T

    def send_rows(it, h):
        mine = rowx.at[it, d, some_lines(h)]
        to_all("dp", d, nd, lambda j, axis: remote(mine, mine, ROW + 2 * it + h, **{axis: j}))

    def row_total(it, first, last):
        total = rowx[it, 0, first:last]
        for j in range(1, nd):
            total = total + rowx[it, j, first:last]
        return total

    def take_rows(it, h):
        wait_bytes(rsem.at[ROW + 2 * it + h], rowx.at[it, pl.ds(0, nd - 1), some_lines(h)])
        return 1.0 / (row_total(it, h * half_lines, (h + 1) * half_lines) * total_rows)

    def row_part(hb, hr):
        span = 64

        def step(i, carry):
            part = pl.ds(hr * half_rows + i * span, span)
            acc = None if hb == 0 else racc[part, :]
            for b in range(hb * half_blocks, (hb + 1) * half_blocks):
                for j in range(lane_chunks):
                    lanes = slice(j * LANES, (j + 1) * LANES)
                    term = e_ref[b, part, lanes] * v_ref[b, :, lanes]
                    acc = term if acc is None else acc + term
            racc[part, :] = acc
            return carry

        lax.fori_loop(0, half_rows // span, step, 0, unroll=True)

    def row_pass(it):
        take_cols(it, 0)
        row_part(0, 0)
        row_part(0, 1)
        take_cols(it, 1)
        for h in range(2):
            row_part(1, h)
            first, last = h * half_lines, (h + 1) * half_lines
            rowx[it, d, first:last] = dense(racc, first, last)
            send_rows(it, h)

    def col_part(it, hr, first, last):
        pair = 2

        def step(b2, carry):
            def inner(i, accs):
                accs = list(accs)
                for g in range(8):
                    part = pl.ds(hr * half_rows + i * 64 + g * 8, 8)
                    r = rb_ref[part, :]
                    for k in range(pair):
                        for j in range(lane_chunks):
                            n = k * lane_chunks + j
                            accs[n] = accs[n] + e_ref[b2 * pair + k, part, j * LANES:(j + 1) * LANES] * r
                return tuple(accs)

            spots = [(b2 * pair + k, slice(j * LANES, (j + 1) * LANES))
                     for k in range(pair) for j in range(lane_chunks)]
            if hr == 0:
                init = (jnp.zeros((8, LANES), F32),) * len(spots)
            else:
                init = tuple(cacc[b, :, lanes] for b, lanes in spots)
            accs = lax.fori_loop(0, half_rows // 64, inner, init, unroll=min(4, half_rows // 64))
            for acc, (b, lanes) in zip(accs, spots):
                if hr == 0:
                    cacc[b, :, lanes] = acc
                else:
                    colx[it, p, b, :, lanes] = jnp.sum(acc, axis=0, keepdims=True)
            return carry

        lax.fori_loop(first // pair, last // pair, step, 0)

    def col_pass(it):
        spread(take_rows(it - 1, 0), rb_ref, 0)
        col_part(it, 0, 0, np_)
        spread(take_rows(it - 1, 1), rb_ref, half_lines)
        for h in range(2):
            col_part(it, 1, h * half_blocks, (h + 1) * half_blocks)
            send_cols(it, h)

    def student_pass(first, last):
        def step(block, carry):
            for i in range(ntiles):
                part = slice(i * tile, (i + 1) * tile)
                dots = jnp.dot(s_all[part, :], w_all[block], preferred_element_type=F32)
                sums = fold_lanes(jnp.exp2(dots * as_ref[block]))
                sacc[part, :] += sums
            return carry
        lax.fori_loop(first, last, step, 0)

    send_cols(0, 0)
    send_cols(0, 1)
    sacc[...] = jnp.zeros_like(sacc)
    row_pass(0)
    wait_bytes(rsem.at[S_GATHER], s_all.at[pl.ds(0, rows - chunk)])
    for c in range(lines):
        s_t[:, c * LANES:(c + 1) * LANES] = s_all[c * LANES:(c + 1) * LANES, :].T
    student_pass(0, 4)
    col_pass(1)
    student_pass(4, 6)
    row_pass(1)
    student_pass(6, 8)
    soft[d] = dense(sacc, 0, lines)
    to_all("dp", d, nd, lambda j, axis: remote(soft.at[d], soft.at[d], SOFT, **{axis: j}))
    col_pass(2)
    wait_bytes(rsem.at[SOFT], soft.at[pl.ds(0, nd - 1)])
    soft_total = soft[0]
    for j in range(1, nd):
        soft_total = soft_total + soft[j]
    spread(1.0 / (soft_total * (total_rows * STUDENT_TEMP)), sb_ref, 0)
    lse = jnp.log(soft_total)
    row_pass(2)
    for h in range(2):
        spread(take_rows(2, h) * (1.0 / STUDENT_TEMP), rb_ref, h * half_lines)

    half_cols = cols // 2

    def unit(block, side, g_tile, acc):
        base = side * half_cols
        columns = slice(base, base + half_cols)
        for i in range(ntiles):
            part = slice(i * tile, (i + 1) * tile)
            zb = jnp.dot(s_all[part, :], w_all[block, :, columns],
                         preferred_element_type=F32) * as_ref[block, :, columns]
            es = jnp.exp2(zb)
            q_scale = rb_ref[part, :]
            p_scale = sb_ref[part, :]
            for j in range(half_cols // LANES):
                lanes = slice(j * LANES, (j + 1) * LANES)
                here = slice(base + j * LANES, base + (j + 1) * LANES)
                q = e_ref[block, part, here] * v_ref[block, :, here] * q_scale
                g_tile[part, lanes] = (es[:, lanes] * p_scale - q).astype(BF16)
                acc = acc + fold_rows(q * zb[:, lanes])
        return acc

    owners = [opposite, plus, minus, p]
    z_copies = {}
    core_copies = {}

    def chip_sum(n, side):
        core_copies[n, side].wait_recv()
        if (n, side) == (1, 0):
            z_copies["a"].wait_recv()
            g_own[n, side] = g_own[n, side] + g_recv[n, side] + half_a[...]
        elif (n, side) == (2, 1):
            z_copies["b"].wait_recv()
            g_own[n, side] = g_own[n, side] + g_recv[n, side] + half_b[...]
        else:
            g_own[n, side] += g_recv[n, side]
        mine = g_own.at[n, side]
        if (n, side) == (0, 0):
            z_copies["a"] = go(remote(mine, half_a, G_HALF_A, proto=plus))
        elif (n, side) == (0, 1):
            z_copies["b"] = go(remote(mine, half_b, G_HALF_B, proto=minus))
        elif n == 1:
            z_copies[0, side] = go(remote(mine, g_z.at[0, side], G_PLUS + side, proto=plus))
        elif n == 2:
            z_copies[1, side] = go(remote(mine, g_z.at[1, side], G_MINUS + side, proto=minus))

    def gradient(n, side, is_own, g_tile):
        dst = g_own if is_own else g_send
        dst[n, side] = jnp.dot(s_t[...], g_tile[...], preferred_element_type=F32)

    order = [(0, 0), (0, 1), (1, 1), (2, 0), (3, 0), (3, 1), (1, 0), (2, 1)]
    units = [(n, side, is_own) for n, side in order for is_own in (False, True)]
    loss_acc = jnp.zeros((8, LANES), F32)
    waiting = None
    for k in range(len(units) + 2):
        if 0 < k <= len(units):
            gradient(*units[k - 1], g_tiles.at[(k - 1) % 2])
        if k < len(units):
            n, side, is_own = units[k]
            block = owners[n] if is_own else other(owners[n])
            loss_acc = unit(block, side, g_tiles.at[k % 2], loss_acc)
        if waiting is not None:
            chip_sum(*waiting)
            waiting = None
        if 0 < k <= len(units):
            n, side, is_own = units[k - 1]
            if is_own:
                waiting = (n, side)
            else:
                core_copies[n, side] = go(remote(
                    g_send.at[n, side], g_recv.at[n, side], G_CORE + 2 * n + side, proto=partner))

    first_line = lax.broadcasted_iota(jnp.int32, (8, LANES), 0) == 0
    lse_sum = jnp.broadcast_to(jnp.sum(lse, axis=0, keepdims=True) * (1.0 / nd), (8, LANES))
    loss_scale = total_rows * STUDENT_TEMP / LOG2E
    loss_p[p] = jnp.where(first_line, lse_sum, 0.0) - loss_acc * loss_scale
    to_all("proto", p, np_, lambda j, axis: remote(
        loss_p.at[p], loss_p.at[p], LOSS_PROTO, **{axis: j}))
    wait_bytes(rsem.at[LOSS_PROTO], loss_p.at[pl.ds(0, np_ - 1)])
    part = loss_p[0]
    for j in range(1, np_):
        part = part + loss_p[j]
    loss_d[d] = part
    to_all("dp", d, nd, lambda j, axis: remote(
        loss_d.at[d], loss_d.at[d], LOSS_DP, **{axis: j}))

    for side in (0, 1):
        columns = slice(side * half_cols, (side + 1) * half_cols)
        z_copies[0, side].wait_recv()
        z_copies[1, side].wait_recv()
        grad = g_own[3, side] + g_z[0, side] + g_z[1, side]
        inv = inv_ref[p, :, columns]
        dirs = w_all[p, :, columns].astype(F32) * inv
        col = jnp.sum(dirs * grad, axis=0, keepdims=True)
        g_own[3, side] = (grad - dirs * col) * inv
        to_all("dp", d, nd, lambda j, axis: remote(
            g_own.at[3, side, pl.ds(j * own_depth, own_depth)], out_recv.at[side, d],
            OUT_A2A + side, **{axis: j}))
        out_recv[side, d] = g_own[3, side, own_rows]

    wait_bytes(rsem.at[LOSS_DP], loss_d.at[pl.ds(0, nd - 1)])
    whole = loss_d[0]
    for j in range(1, nd):
        whole = whole + loss_d[j]
    loss_out[0, 0] = jnp.sum(whole) * (1.0 / total_rows)

    for side in (0, 1):
        wait_bytes(rsem.at[OUT_A2A + side], out_recv.at[side, pl.ds(0, nd - 1)])
        for j in range(nd):
            base = j * cols + side * half_cols
            out[:, base:base + half_cols] = out_recv[side, j]

    for copy in copies:
        if copy is not up_top and copy is not down_bottom:
            copy.wait_send()
    wait_bytes(ssem.at[W_A2A], w_all.at[0, pl.ds(0, depth - own_depth)])
    wait_bytes(ssem.at[T_GATHER], t_all.at[pl.ds(0, rows - chunk)])
    wait_bytes(ssem.at[S_GATHER], s_all.at[pl.ds(0, rows - chunk)])
    for it in range(ITERS):
        for h in range(2):
            wait_bytes(ssem.at[COL + 2 * it + h], colx.at[it, pl.ds(0, np_ - 1), some_blocks(h)])
            wait_bytes(ssem.at[ROW + 2 * it + h], rowx.at[it, pl.ds(0, nd - 1), some_lines(h)])
    wait_bytes(ssem.at[SOFT], soft.at[pl.ds(0, nd - 1)])
    for side in (0, 1):
        wait_bytes(ssem.at[OUT_A2A + side], out_recv.at[side, pl.ds(0, nd - 1)])
    wait_bytes(ssem.at[LOSS_PROTO], loss_p.at[pl.ds(0, np_ - 1)])
    wait_bytes(ssem.at[LOSS_DP], loss_d.at[pl.ds(0, nd - 1)])


def body(nd, np_, teacher_feat, student_feat, proto_weight):
    block_rows, depth = teacher_feat.shape
    own_depth, block_cols = proto_weight.shape
    chunk, cols = block_rows // np_, block_cols // nd
    rows = chunk * nd
    tile = min(256, rows)
    vmem = pltpu.VMEM
    out, loss = pl.pallas_call(
        functools.partial(kernel, nd, np_, tile),
        out_shape=(
            jax.ShapeDtypeStruct((own_depth, block_cols), F32),
            jax.ShapeDtypeStruct((1, 1), F32),
        ),
        in_specs=[pl.BlockSpec(memory_space=pl.ANY)] * 3,
        out_specs=[pl.BlockSpec(memory_space=vmem), pl.BlockSpec(memory_space=pltpu.SMEM)],
        scratch_shapes=[
            vmem((chunk, depth), BF16),
            vmem((chunk, depth), BF16),
            vmem((rows, depth), BF16),
            vmem((rows, depth), BF16),
            vmem((depth, rows), BF16),
            vmem((np_, depth, cols), BF16),
            vmem((np_, rows, cols), F32),
            vmem((np_, 1, cols), F32),
            vmem((np_, 1, cols), F32),
            vmem((np_, 1, cols), F32),
            vmem((np_, 1, cols), F32),
            vmem((rows, LANES), F32),
            vmem((rows, LANES), F32),
            vmem((rows, LANES), F32),
            vmem((rows, LANES), F32),
            vmem((np_, 8, cols), F32),
            vmem((ITERS, np_, np_, 1, cols), F32),
            vmem((ITERS, nd, rows // LANES, LANES), F32),
            vmem((nd, rows // LANES, LANES), F32),
            vmem((2, rows, cols // 2), BF16),
            vmem((4, 2, depth, cols // 2), F32),
            vmem((4, 2, depth, cols // 2), F32),
            vmem((4, 2, depth, cols // 2), F32),
            vmem((depth, cols // 2), F32),
            vmem((depth, cols // 2), F32),
            vmem((2, 2, depth, cols // 2), F32),
            vmem((2, nd, own_depth, cols // 2), F32),
            vmem((np_, 8, LANES), F32),
            vmem((nd, 8, LANES), F32),
            pltpu.SemaphoreType.DMA((STAGES,)),
            pltpu.SemaphoreType.DMA((STAGES,)),
            pltpu.SemaphoreType.DMA((3,)),
        ],
        compiler_params=pltpu.CompilerParams(
            collective_id=0, has_side_effects=True, vmem_limit_bytes=62 * 1024 * 1024),
        cost_estimate=pl.CostEstimate(
            flops=6 * rows * cols * np_ * depth, bytes_accessed=2 ** 21,
            transcendentals=2 * rows * cols * np_),
    )(teacher_feat, student_feat, proto_weight)
    return out, jnp.reshape(loss, ())


def solution(mesh):
    nd, np_ = mesh.shape["dp"], mesh.shape["proto"]
    in_specs = (P("dp", None), P("dp", None), P("dp", "proto"))
    out_specs = (P("dp", "proto"), P())
    return jax.shard_map(
        functools.partial(body, nd, np_), mesh=mesh, in_specs=in_specs, out_specs=out_specs, check_vma=False)
```

```python
import functools
import math

import jax
import jax.numpy as jnp
from jax import lax
from jax.experimental import pallas as pl
from jax.experimental.pallas import tpu as pltpu
from jax.sharding import PartitionSpec as P

ITERS = 3
EPS = 1e-06
TEACHER_TEMP = 0.07
STUDENT_TEMP = 0.1
LOG2E = math.log2(math.e)
LANES = 128
MESH = pl.DeviceIdType.MESH
F32 = jnp.float32
BF16 = jnp.bfloat16

W_A2A, T_GATHER, S_GATHER = 0, 1, 2
SOFT = 3
LOSS_PROTO, LOSS_DP = 4, 5
W_PLUS, W_MINUS = 6, 8
W_HALF_A, W_HALF_B = 10, 11
W_CORE = 16
G_CORE = 20
G_HALF_A, G_HALF_B = 28, 29
G_PLUS, G_MINUS = 30, 31
G_LAST = 32
OUT_A2A = 48
COL = 36
ROW = 42
STAGES = 52


def unit_rows(feat):
    values = feat.astype(F32)
    scaled = values / jnp.sqrt(jnp.sum(values * values, axis=1, keepdims=True) + EPS)
    return scaled.astype(BF16)


def fold_rows(x):
    n, c = x.shape
    return jnp.sum(x.reshape(n // 8, 8, c), axis=0)


def fold_lanes(x):
    total = x[:, :LANES]
    for j in range(1, x.shape[1] // LANES):
        total = total + x[:, j * LANES:(j + 1) * LANES]
    return total


def kernel(
    nd, np_, tile,
    teacher, student, weight,
    out, loss_out,
    t_raw, s_raw, t_all, s_all, s_t, w_all, e_ref,
    at_ref, as_ref, inv_ref, v_ref, rb_ref, sb_ref, racc, sacc,
    cacc, colx, rowx, soft, g_tiles, g_send, g_recv, g_own, half_a, half_b, g_z, out_send, out_recv,
    loss_p, loss_d,
    ssem, rsem, lsem,
):
    d = lax.axis_index("dp")
    p = lax.axis_index("proto")
    nz = np_ // 2
    partner = p + 1 - 2 * lax.rem(p, 2)
    plus = lax.rem(p + 2, np_)
    minus = lax.rem(p + np_ - 2, np_)
    chunk = t_raw.shape[0]
    rows = t_all.shape[0]
    depth, cols = w_all.shape[1:]
    own_depth = depth // nd
    ntiles = rows // tile
    total_rows = rows * np_
    total_cols = cols * np_ * nd

    def other(block):
        return block + 1 - 2 * lax.rem(block, 2)

    def remote(src, dst, stage, **where):
        return pltpu.make_async_remote_copy(
            src_ref=src, dst_ref=dst, send_sem=ssem.at[stage], recv_sem=rsem.at[stage],
            device_id=where, device_id_type=MESH)

    def to_all(axis, me, n, make):
        def step(o, carry):
            make(lax.rem(me + o, n), axis).start()
            return carry
        lax.fori_loop(1, n, step, 0)

    def wait_bytes(sem, ref):
        pltpu.make_async_copy(ref, ref, sem).wait()

    barrier = pltpu.get_barrier_semaphore()

    def greet(axis, me, n):
        def step(o, carry):
            pl.semaphore_signal(barrier, inc=1, device_id={axis: lax.rem(me + o, n)}, device_id_type=MESH)
            return carry
        lax.fori_loop(1, n, step, 0)

    greet("dp", d, nd)
    greet("proto", p, np_)

    load_t = pltpu.make_async_copy(teacher.at[pl.ds(p * chunk, chunk)], t_raw, lsem.at[0])
    load_s = pltpu.make_async_copy(student.at[pl.ds(p * chunk, chunk)], s_raw, lsem.at[1])
    own_rows = pl.ds(d * own_depth, own_depth)
    load_w = pltpu.make_async_copy(
        weight.at[:, pl.ds(d * cols, cols)], w_all.at[p, own_rows], lsem.at[2])
    load_t.start()
    load_s.start()
    load_w.start()
    load_t.wait()
    own_chunk = pl.ds(d * chunk, chunk)
    t_all[own_chunk, :] = unit_rows(t_raw[...])
    pl.semaphore_wait(barrier, nd + np_ - 2)

    to_all("dp", d, nd, lambda j, axis: remote(
        weight.at[:, pl.ds(j * cols, cols)], w_all.at[p, own_rows], W_A2A, **{axis: j}))
    load_s.wait()
    s_all[own_chunk, :] = unit_rows(s_raw[...])

    load_w.wait()
    wait_bytes(rsem.at[W_A2A], w_all.at[p, pl.ds(0, depth - own_depth)])
    half = depth // 2
    top, bottom = pl.ds(0, half), pl.ds(half, half)
    copies = []

    def go(copy):
        copy.start()
        copies.append(copy)
        return copy

    opposite = lax.rem(p + 4, np_)
    def ring(part, stage, to):
        return remote(w_all.at[p, part], w_all.at[p, part], stage, proto=to)

    up_top = go(ring(top, W_PLUS, plus))
    down_bottom = go(ring(bottom, W_MINUS, minus))
    core = [None] * 4
    core[0] = go(remote(w_all.at[p], w_all.at[p], W_CORE, proto=partner))
    to_all("dp", d, nd, lambda j, axis: remote(
        t_all.at[own_chunk], t_all.at[own_chunk], T_GATHER, **{axis: j}))
    up_bottom = go(ring(bottom, W_PLUS + 1, plus))
    down_top = go(ring(top, W_MINUS + 1, minus))
    up_top.wait_recv()
    pass_a = go(remote(w_all.at[minus, top], w_all.at[minus, top], W_HALF_A, proto=plus))
    down_bottom.wait_recv()
    pass_b = go(remote(w_all.at[plus, bottom], w_all.at[plus, bottom], W_HALF_B, proto=minus))
    up_bottom.wait_recv()
    core[1] = go(remote(w_all.at[minus], w_all.at[minus], W_CORE + 1, proto=partner))
    down_top.wait_recv()
    core[2] = go(remote(w_all.at[plus], w_all.at[plus], W_CORE + 2, proto=partner))

    wait_bytes(rsem.at[T_GATHER], t_all.at[pl.ds(0, rows - chunk)])
    to_all("dp", d, nd, lambda j, axis: remote(
        s_all.at[own_chunk], s_all.at[own_chunk], S_GATHER, **{axis: j}))

    def first_pass(block):
        w = w_all[block].astype(F32)
        inv = 1.0 / jnp.sqrt(jnp.sum(w * w, axis=0, keepdims=True) + EPS)
        inv_ref[block] = inv
        at_ref[block] = inv * (LOG2E / TEACHER_TEMP)
        as_ref[block] = inv * (LOG2E / STUDENT_TEMP)

        acc = jnp.zeros((8, cols), F32)
        for i in range(ntiles):
            part = slice(i * tile, (i + 1) * tile)
            dots = jnp.dot(t_all[part, :], w_all[block], preferred_element_type=F32)
            e = jnp.exp2(dots * at_ref[block])
            e_ref[block, part, :] = e
            acc = acc + fold_rows(e)
        colx[0, p, block] = jnp.sum(acc, axis=0, keepdims=True)

    first_pass(p)
    core[0].wait_recv()
    first_pass(partner)
    first_pass(minus)
    first_pass(plus)
    core[1].wait_recv()
    first_pass(other(minus))
    core[2].wait_recv()
    first_pass(other(plus))
    pass_a.wait_recv()
    pass_b.wait_recv()
    core[3] = go(remote(w_all.at[opposite], w_all.at[opposite], W_CORE + 3, proto=partner))
    first_pass(opposite)
    core[3].wait_recv()
    first_pass(other(opposite))

    half_blocks, half_rows = np_ // 2, rows // 2
    lines = rows // LANES
    half_lines = lines // 2
    lane_chunks = cols // LANES

    def some_blocks(h):
        return pl.ds(h * half_blocks, half_blocks)

    def some_lines(h):
        return pl.ds(h * half_lines, half_lines)

    def send_cols(it, h):
        mine = colx.at[it, p, some_blocks(h)]
        to_all("proto", p, np_, lambda j, axis: remote(mine, mine, COL + 2 * it + h, **{axis: j}))

    def take_cols(it, h):
        wait_bytes(rsem.at[COL + 2 * it + h], colx.at[it, pl.ds(0, np_ - 1), some_blocks(h)])
        mass = colx[it, 0, some_blocks(h)]
        for j in range(1, np_):
            mass = mass + colx[it, j, some_blocks(h)]
        v_ref[some_blocks(h)] = 1.0 / (mass * total_cols)

    def dense(acc_ref, first, last):
        sums = [
            jnp.sum(acc_ref[c * LANES:(c + 1) * LANES, :].T, axis=0, keepdims=True)
            for c in range(first, last)]
        return jnp.concatenate(sums, axis=0)

    def spread(x, ref, first):
        for c in range(x.shape[0]):
            at = (first + c) * LANES
            ref[at:at + LANES, :] = jnp.broadcast_to(x[c:c + 1, :], (LANES, LANES)).T

    def send_rows(it, h):
        mine = rowx.at[it, d, some_lines(h)]
        to_all("dp", d, nd, lambda j, axis: remote(mine, mine, ROW + 2 * it + h, **{axis: j}))

    def row_total(it, first, last):
        total = rowx[it, 0, first:last]
        for j in range(1, nd):
            total = total + rowx[it, j, first:last]
        return total

    def take_rows(it, h):
        wait_bytes(rsem.at[ROW + 2 * it + h], rowx.at[it, pl.ds(0, nd - 1), some_lines(h)])
        return 1.0 / (row_total(it, h * half_lines, (h + 1) * half_lines) * total_rows)

    def row_part(hb, hr):
        span = 64

        def step(i, carry):
            part = pl.ds(hr * half_rows + i * span, span)
            acc = None if hb == 0 else racc[part, :]
            for b in range(hb * half_blocks, (hb + 1) * half_blocks):
                for j in range(lane_chunks):
                    lanes = slice(j * LANES, (j + 1) * LANES)
                    term = e_ref[b, part, lanes] * v_ref[b, :, lanes]
                    acc = term if acc is None else acc + term
            racc[part, :] = acc
            return carry

        lax.fori_loop(0, half_rows // span, step, 0, unroll=True)

    def row_pass(it):
        take_cols(it, 0)
        row_part(0, 0)
        row_part(0, 1)
        take_cols(it, 1)
        for h in range(2):
            row_part(1, h)
            first, last = h * half_lines, (h + 1) * half_lines
            rowx[it, d, first:last] = dense(racc, first, last)
            send_rows(it, h)

    def col_part(it, hr, first, last):
        pair = 2

        def step(b2, carry):
            def inner(i, accs):
                accs = list(accs)
                for g in range(8):
                    part = pl.ds(hr * half_rows + i * 64 + g * 8, 8)
                    r = rb_ref[part, :]
                    for k in range(pair):
                        for j in range(lane_chunks):
                            n = k * lane_chunks + j
                            accs[n] = accs[n] + e_ref[b2 * pair + k, part, j * LANES:(j + 1) * LANES] * r
                return tuple(accs)

            spots = [(b2 * pair + k, slice(j * LANES, (j + 1) * LANES))
                     for k in range(pair) for j in range(lane_chunks)]
            if hr == 0:
                init = (jnp.zeros((8, LANES), F32),) * len(spots)
            else:
                init = tuple(cacc[b, :, lanes] for b, lanes in spots)
            accs = lax.fori_loop(0, half_rows // 64, inner, init, unroll=min(4, half_rows // 64))
            for acc, (b, lanes) in zip(accs, spots):
                if hr == 0:
                    cacc[b, :, lanes] = acc
                else:
                    colx[it, p, b, :, lanes] = jnp.sum(acc, axis=0, keepdims=True)
            return carry

        lax.fori_loop(first // pair, last // pair, step, 0)

    def col_pass(it):
        spread(take_rows(it - 1, 0), rb_ref, 0)
        col_part(it, 0, 0, np_)
        spread(take_rows(it - 1, 1), rb_ref, half_lines)
        for h in range(2):
            col_part(it, 1, h * half_blocks, (h + 1) * half_blocks)
            send_cols(it, h)

    def student_pass(first, last):
        def step(block, carry):
            for i in range(ntiles):
                part = slice(i * tile, (i + 1) * tile)
                dots = jnp.dot(s_all[part, :], w_all[block], preferred_element_type=F32)
                sums = fold_lanes(jnp.exp2(dots * as_ref[block]))
                sacc[part, :] += sums
            return carry
        lax.fori_loop(first, last, step, 0)

    send_cols(0, 0)
    send_cols(0, 1)
    sacc[...] = jnp.zeros_like(sacc)
    row_pass(0)
    wait_bytes(rsem.at[S_GATHER], s_all.at[pl.ds(0, rows - chunk)])
    for c in range(lines):
        s_t[:, c * LANES:(c + 1) * LANES] = s_all[c * LANES:(c + 1) * LANES, :].T
    student_pass(0, 4)
    col_pass(1)
    student_pass(4, 6)
    row_pass(1)
    student_pass(6, 8)
    soft[d] = dense(sacc, 0, lines)
    to_all("dp", d, nd, lambda j, axis: remote(soft.at[d], soft.at[d], SOFT, **{axis: j}))
    col_pass(2)
    wait_bytes(rsem.at[SOFT], soft.at[pl.ds(0, nd - 1)])
    soft_total = soft[0]
    for j in range(1, nd):
        soft_total = soft_total + soft[j]
    spread(1.0 / (soft_total * (total_rows * STUDENT_TEMP)), sb_ref, 0)
    lse = jnp.log(soft_total)
    row_pass(2)
    for h in range(2):
        spread(take_rows(2, h) * (1.0 / STUDENT_TEMP), rb_ref, h * half_lines)

    half_cols, quarter_cols = cols // 2, cols // 4

    def unit(block, side, g_tile, acc):
        base = side * half_cols
        columns = slice(base, base + half_cols)
        for i in range(ntiles):
            part = slice(i * tile, (i + 1) * tile)
            zb = jnp.dot(s_all[part, :], w_all[block, :, columns],
                         preferred_element_type=F32) * as_ref[block, :, columns]
            es = jnp.exp2(zb)
            q_scale = rb_ref[part, :]
            p_scale = sb_ref[part, :]
            for j in range(half_cols // LANES):
                lanes = slice(j * LANES, (j + 1) * LANES)
                here = slice(base + j * LANES, base + (j + 1) * LANES)
                q = e_ref[block, part, here] * v_ref[block, :, here] * q_scale
                g_tile[part, lanes] = (es[:, lanes] * p_scale - q).astype(BF16)
                acc = acc + fold_rows(q * zb[:, lanes])
        return acc

    owners = [opposite, plus, minus, p]
    z_copies = {}
    core_copies = {}

    def chip_sum(n, side):
        core_copies[n, side].wait_recv()
        if (n, side) == (1, 0):
            z_copies["a"].wait_recv()
            g_own[n, side] = g_own[n, side] + g_recv[n, side] + half_a[...]
        elif (n, side) == (2, 1):
            z_copies["b"].wait_recv()
            g_own[n, side] = g_own[n, side] + g_recv[n, side] + half_b[...]
        else:
            g_own[n, side] += g_recv[n, side]
        mine = g_own.at[n, side]
        if (n, side) == (0, 0):
            z_copies["a"] = go(remote(mine, half_a, G_HALF_A, proto=plus))
        elif (n, side) == (0, 1):
            z_copies["b"] = go(remote(mine, half_b, G_HALF_B, proto=minus))
        elif (n, side) == (1, 1):
            z_copies["plus"] = go(remote(mine, g_z.at[0, 1], G_PLUS, proto=plus))
        elif (n, side) == (2, 0):
            z_copies["minus"] = go(remote(mine, g_z.at[1, 0], G_MINUS, proto=minus))
        elif n != 3:
            send_last(side, 0)

    def send_last(side, quarter):
        lanes = pl.ds(quarter * quarter_cols, quarter_cols)
        to = plus if side == 0 else minus
        z_copies[side, quarter] = go(remote(
            g_own.at[side + 1, side, :, lanes], g_z.at[side, side, :, lanes],
            G_LAST + 2 * quarter + side, proto=to))

    def gradient(n, side, is_own, g_tile):
        dst = g_own if is_own else g_send
        dst[n, side] = jnp.dot(s_t[...], g_tile[...], preferred_element_type=F32)

    def send_core(n, side):
        core_copies[n, side] = go(remote(
            g_send.at[n, side], g_recv.at[n, side], G_CORE + 2 * n + side, proto=partner))

    order = [(0, 0), (0, 1), (1, 1), (2, 0), (3, 0), (3, 1), (1, 0), (2, 1)]
    units = [(n, side, is_own) for n, side in order for is_own in (False, True)]
    loss_acc = jnp.zeros((8, LANES), F32)
    waiting = None
    for k in range(len(units) + 2):
        if 2 < k <= len(units):
            gradient(*units[k - 1], g_tiles.at[(k - 1) % 2])
        if k < len(units):
            n, side, is_own = units[k]
            block = owners[n] if is_own else other(owners[n])
            loss_acc = unit(block, side, g_tiles.at[k % 2], loss_acc)
        if k < 2:
            gradient(*units[k], g_tiles.at[k % 2])
        if k == 0:
            send_core(*units[0][:2])
        elif k == 1:
            chip_sum(*units[1][:2])
        if waiting is not None:
            chip_sum(*waiting)
            waiting = None
        if 2 < k <= len(units):
            if units[k - 1][2]:
                waiting = units[k - 1][:2]
            else:
                send_core(*units[k - 1][:2])
    first_quarters = [z_copies[0, 0], z_copies[1, 0]]
    for side in (0, 1):
        send_last(side, 1)

    first_line = lax.broadcasted_iota(jnp.int32, (8, LANES), 0) == 0
    lse_sum = jnp.broadcast_to(jnp.sum(lse, axis=0, keepdims=True) * (1.0 / nd), (8, LANES))
    loss_scale = total_rows * STUDENT_TEMP / LOG2E
    loss_d[d] = jnp.where(first_line, lse_sum, 0.0) - loss_acc * loss_scale
    to_all("dp", d, nd, lambda j, axis: remote(
        loss_d.at[d], loss_d.at[d], LOSS_DP, **{axis: j}))
    wait_bytes(rsem.at[LOSS_DP], loss_d.at[pl.ds(0, nd - 1)])
    part = loss_d[0]
    for j in range(1, nd):
        part = part + loss_d[j]
    loss_p[p] = part
    to_all("proto", p, np_, lambda j, axis: remote(
        loss_p.at[p], loss_p.at[p], LOSS_PROTO, **{axis: j}))

    for quarter in (0, 1):
        lanes = slice(quarter * quarter_cols, (quarter + 1) * quarter_cols)
        for side in (0, 1):
            if quarter == 0:
                z_copies["minus" if side == 0 else "plus"].wait_recv()
            z_copies[side, quarter].wait_recv()
            n = 2 * quarter + side
            columns = slice(side * half_cols + lanes.start, side * half_cols + lanes.stop)
            grad = g_own[3, side, :, lanes] + g_z[0, side, :, lanes] + g_z[1, side, :, lanes]
            inv = inv_ref[p, :, columns]
            dirs = w_all[p, :, columns].astype(F32) * inv
            col = jnp.sum(dirs * grad, axis=0, keepdims=True)
            out_send[n] = (grad - dirs * col) * inv
            to_all("dp", d, nd, lambda j, axis: remote(
                out_send.at[n, pl.ds(j * own_depth, own_depth)], out_recv.at[n, d],
                OUT_A2A + n, **{axis: j}))
            out_recv[n, d] = out_send[n, own_rows]

    for n in range(4):
        wait_bytes(rsem.at[OUT_A2A + n], out_recv.at[n, pl.ds(0, nd - 1)])
        for j in range(nd):
            base = j * cols + (n % 2) * half_cols + (n // 2) * quarter_cols
            out[:, base:base + quarter_cols] = out_recv[n, j]

    wait_bytes(rsem.at[LOSS_PROTO], loss_p.at[pl.ds(0, np_ - 1)])
    whole = loss_p[0]
    for j in range(1, np_):
        whole = whole + loss_p[j]
    loss_out[0, 0] = jnp.sum(whole) * (1.0 / total_rows)

    for copy in copies:
        copy.wait_send()
    wait_bytes(ssem.at[W_A2A], w_all.at[0, pl.ds(0, depth - own_depth)])
    wait_bytes(ssem.at[T_GATHER], t_all.at[pl.ds(0, rows - chunk)])
    wait_bytes(ssem.at[S_GATHER], s_all.at[pl.ds(0, rows - chunk)])
    for it in range(ITERS):
        for h in range(2):
            wait_bytes(ssem.at[COL + 2 * it + h], colx.at[it, pl.ds(0, np_ - 1), some_blocks(h)])
            wait_bytes(ssem.at[ROW + 2 * it + h], rowx.at[it, pl.ds(0, nd - 1), some_lines(h)])
    wait_bytes(ssem.at[SOFT], soft.at[pl.ds(0, nd - 1)])
    for n in range(4):
        wait_bytes(ssem.at[OUT_A2A + n], out_recv.at[n, pl.ds(0, nd - 1)])
    wait_bytes(ssem.at[LOSS_PROTO], loss_p.at[pl.ds(0, np_ - 1)])
    wait_bytes(ssem.at[LOSS_DP], loss_d.at[pl.ds(0, nd - 1)])


def body(nd, np_, teacher_feat, student_feat, proto_weight):
    block_rows, depth = teacher_feat.shape
    own_depth, block_cols = proto_weight.shape
    chunk, cols = block_rows // np_, block_cols // nd
    rows = chunk * nd
    tile = min(256, rows)
    vmem = pltpu.VMEM
    out, loss = pl.pallas_call(
        functools.partial(kernel, nd, np_, tile),
        out_shape=(
            jax.ShapeDtypeStruct((own_depth, block_cols), F32),
            jax.ShapeDtypeStruct((1, 1), F32),
        ),
        in_specs=[pl.BlockSpec(memory_space=pl.ANY)] * 3,
        out_specs=[pl.BlockSpec(memory_space=vmem), pl.BlockSpec(memory_space=pltpu.SMEM)],
        scratch_shapes=[
            vmem((chunk, depth), BF16),
            vmem((chunk, depth), BF16),
            vmem((rows, depth), BF16),
            vmem((rows, depth), BF16),
            vmem((depth, rows), BF16),
            vmem((np_, depth, cols), BF16),
            vmem((np_, rows, cols), F32),
            vmem((np_, 1, cols), F32),
            vmem((np_, 1, cols), F32),
            vmem((np_, 1, cols), F32),
            vmem((np_, 1, cols), F32),
            vmem((rows, LANES), F32),
            vmem((rows, LANES), F32),
            vmem((rows, LANES), F32),
            vmem((rows, LANES), F32),
            vmem((np_, 8, cols), F32),
            vmem((ITERS, np_, np_, 1, cols), F32),
            vmem((ITERS, nd, rows // LANES, LANES), F32),
            vmem((nd, rows // LANES, LANES), F32),
            vmem((2, rows, cols // 2), BF16),
            vmem((4, 2, depth, cols // 2), F32),
            vmem((4, 2, depth, cols // 2), F32),
            vmem((4, 2, depth, cols // 2), F32),
            vmem((depth, cols // 2), F32),
            vmem((depth, cols // 2), F32),
            vmem((2, 2, depth, cols // 2), F32),
            vmem((4, depth, cols // 4), F32),
            vmem((4, nd, own_depth, cols // 4), F32),
            vmem((np_, 8, LANES), F32),
            vmem((nd, 8, LANES), F32),
            pltpu.SemaphoreType.DMA((STAGES,)),
            pltpu.SemaphoreType.DMA((STAGES,)),
            pltpu.SemaphoreType.DMA((3,)),
        ],
        compiler_params=pltpu.CompilerParams(
            collective_id=0, has_side_effects=True, vmem_limit_bytes=62 * 1024 * 1024),
        cost_estimate=pl.CostEstimate(
            flops=6 * rows * cols * np_ * depth, bytes_accessed=2 ** 21,
            transcendentals=2 * rows * cols * np_),
    )(teacher_feat, student_feat, proto_weight)
    return out, jnp.reshape(loss, ())


def solution(mesh):
    nd, np_ = mesh.shape["dp"], mesh.shape["proto"]
    in_specs = (P("dp", None), P("dp", None), P("dp", "proto"))
    out_specs = (P("dp", "proto"), P())
    return jax.shard_map(
        functools.partial(body, nd, np_), mesh=mesh, in_specs=in_specs, out_specs=out_specs, check_vma=False)
```

```python
import functools
import math

import jax
import jax.numpy as jnp
from jax import lax
from jax.experimental import pallas as pl
from jax.experimental.pallas import tpu as pltpu
from jax.sharding import PartitionSpec as P

ITERS = 3
EPS = 1e-06
TEACHER_TEMP = 0.07
STUDENT_TEMP = 0.1
LOG2E = math.log2(math.e)
LANES = 128
MESH = pl.DeviceIdType.MESH
F32 = jnp.float32
BF16 = jnp.bfloat16

W_A2A, T_GATHER, S_GATHER = 0, 1, 2
SOFT = 3
LOSS_PROTO, LOSS_DP = 4, 5
W_PLUS, W_MINUS = 6, 8
W_HALF_A, W_HALF_B = 10, 11
W_CORE = 16
G_CORE = 20
G_HALF_A, G_HALF_B = 28, 29
G_PLUS, G_MINUS = 30, 31
G_LAST = 32
OUT_A2A = 48
COL = 36
ROW = 42
STAGES = 52


def unit_rows(feat):
    values = feat.astype(F32)
    scaled = values / jnp.sqrt(jnp.sum(values * values, axis=1, keepdims=True) + EPS)
    return scaled.astype(BF16)


def fold_rows(x):
    n, c = x.shape
    return jnp.sum(x.reshape(n // 8, 8, c), axis=0)


def fold_lanes(x):
    total = x[:, :LANES]
    for j in range(1, x.shape[1] // LANES):
        total = total + x[:, j * LANES:(j + 1) * LANES]
    return total


def kernel(
    nd, np_, tile,
    teacher, student, weight,
    out, loss_out,
    t_raw, s_raw, w_raw, t_all, s_all, s_t, w_all, e_ref,
    at_ref, as_ref, inv_ref, v_ref, rb_ref, sb_ref, racc, sacc,
    cacc, colx, rowx, soft, g_tiles, g_send, g_recv, g_own, half_a, half_b, g_z, out_send, out_recv,
    loss_p, loss_d,
    ssem, rsem, lsem,
):
    d = lax.axis_index("dp")
    p = lax.axis_index("proto")
    nz = np_ // 2
    partner = p + 1 - 2 * lax.rem(p, 2)
    plus = lax.rem(p + 2, np_)
    minus = lax.rem(p + np_ - 2, np_)
    chunk = t_raw.shape[0]
    rows = t_all.shape[0]
    depth, cols = w_all.shape[1:]
    own_depth = depth // nd
    ntiles = rows // tile
    total_rows = rows * np_
    total_cols = cols * np_ * nd

    def other(block):
        return block + 1 - 2 * lax.rem(block, 2)

    def remote(src, dst, stage, **where):
        return pltpu.make_async_remote_copy(
            src_ref=src, dst_ref=dst, send_sem=ssem.at[stage], recv_sem=rsem.at[stage],
            device_id=where, device_id_type=MESH)

    def to_all(axis, me, n, make):
        def step(o, carry):
            make(lax.rem(me + o, n), axis).start()
            return carry
        lax.fori_loop(1, n, step, 0)

    def wait_bytes(sem, ref):
        pltpu.make_async_copy(ref, ref, sem).wait()

    barrier = pltpu.get_barrier_semaphore()

    def greet(axis, me, n):
        def step(o, carry):
            pl.semaphore_signal(barrier, inc=1, device_id={axis: lax.rem(me + o, n)}, device_id_type=MESH)
            return carry
        lax.fori_loop(1, n, step, 0)

    greet("dp", d, nd)
    greet("proto", p, np_)

    load_t = pltpu.make_async_copy(teacher.at[pl.ds(p * chunk, chunk)], t_raw, lsem.at[0])
    load_s = pltpu.make_async_copy(student.at[pl.ds(p * chunk, chunk)], s_raw, lsem.at[1])
    own_rows = pl.ds(d * own_depth, own_depth)
    load_w = pltpu.make_async_copy(
        w_raw.at[:, pl.ds(d * cols, cols)], w_all.at[p, own_rows], lsem.at[2])
    load_raw = pltpu.make_async_copy(weight, w_raw, lsem.at[3])
    load_t.start()
    load_raw.start()
    load_s.start()
    load_t.wait()
    own_chunk = pl.ds(d * chunk, chunk)
    t_all[own_chunk, :] = unit_rows(t_raw[...])
    load_raw.wait()
    load_w.start()
    pl.semaphore_wait(barrier, nd + np_ - 2)

    to_all("dp", d, nd, lambda j, axis: remote(
        w_raw.at[:, pl.ds(j * cols, cols)], w_all.at[p, own_rows], W_A2A, **{axis: j}))
    load_s.wait()
    s_all[own_chunk, :] = unit_rows(s_raw[...])

    load_w.wait()
    wait_bytes(rsem.at[W_A2A], w_all.at[p, pl.ds(0, depth - own_depth)])
    half = depth // 2
    top, bottom = pl.ds(0, half), pl.ds(half, half)
    copies = []

    def go(copy):
        copy.start()
        copies.append(copy)
        return copy

    opposite = lax.rem(p + 4, np_)
    def ring(part, stage, to):
        return remote(w_all.at[p, part], w_all.at[p, part], stage, proto=to)

    up_top = go(ring(top, W_PLUS, plus))
    down_bottom = go(ring(bottom, W_MINUS, minus))
    core = [None] * 4
    core[0] = go(remote(w_all.at[p], w_all.at[p], W_CORE, proto=partner))
    to_all("dp", d, nd, lambda j, axis: remote(
        t_all.at[own_chunk], t_all.at[own_chunk], T_GATHER, **{axis: j}))
    up_bottom = go(ring(bottom, W_PLUS + 1, plus))
    down_top = go(ring(top, W_MINUS + 1, minus))
    up_top.wait_recv()
    pass_a = go(remote(w_all.at[minus, top], w_all.at[minus, top], W_HALF_A, proto=plus))
    down_bottom.wait_recv()
    pass_b = go(remote(w_all.at[plus, bottom], w_all.at[plus, bottom], W_HALF_B, proto=minus))
    up_bottom.wait_recv()
    core[1] = go(remote(w_all.at[minus], w_all.at[minus], W_CORE + 1, proto=partner))
    down_top.wait_recv()
    core[2] = go(remote(w_all.at[plus], w_all.at[plus], W_CORE + 2, proto=partner))

    wait_bytes(rsem.at[T_GATHER], t_all.at[pl.ds(0, rows - chunk)])
    to_all("dp", d, nd, lambda j, axis: remote(
        s_all.at[own_chunk], s_all.at[own_chunk], S_GATHER, **{axis: j}))

    def first_pass(block):
        w = w_all[block].astype(F32)
        inv = 1.0 / jnp.sqrt(jnp.sum(w * w, axis=0, keepdims=True) + EPS)
        inv_ref[block] = inv
        at_ref[block] = inv * (LOG2E / TEACHER_TEMP)
        as_ref[block] = inv * (LOG2E / STUDENT_TEMP)

        acc = jnp.zeros((8, cols), F32)
        for i in range(ntiles):
            part = slice(i * tile, (i + 1) * tile)
            dots = jnp.dot(t_all[part, :], w_all[block], preferred_element_type=F32)
            e = jnp.exp2(dots * at_ref[block])
            e_ref[block, part, :] = e
            acc = acc + fold_rows(e)
        colx[0, p, block] = jnp.sum(acc, axis=0, keepdims=True)

    first_pass(p)
    core[0].wait_recv()
    first_pass(partner)
    first_pass(minus)
    first_pass(plus)
    core[1].wait_recv()
    first_pass(other(minus))
    core[2].wait_recv()
    first_pass(other(plus))
    pass_a.wait_recv()
    pass_b.wait_recv()
    core[3] = go(remote(w_all.at[opposite], w_all.at[opposite], W_CORE + 3, proto=partner))
    first_pass(opposite)
    core[3].wait_recv()
    first_pass(other(opposite))

    half_blocks, half_rows = np_ // 2, rows // 2
    lines = rows // LANES
    half_lines = lines // 2
    lane_chunks = cols // LANES

    def some_blocks(h):
        return pl.ds(h * half_blocks, half_blocks)

    def some_lines(h):
        return pl.ds(h * half_lines, half_lines)

    def send_cols(it, h):
        mine = colx.at[it, p, some_blocks(h)]
        to_all("proto", p, np_, lambda j, axis: remote(mine, mine, COL + 2 * it + h, **{axis: j}))

    def take_cols(it, h):
        wait_bytes(rsem.at[COL + 2 * it + h], colx.at[it, pl.ds(0, np_ - 1), some_blocks(h)])
        mass = colx[it, 0, some_blocks(h)]
        for j in range(1, np_):
            mass = mass + colx[it, j, some_blocks(h)]
        v_ref[some_blocks(h)] = 1.0 / (mass * total_cols)

    def dense(acc_ref, first, last):
        sums = [
            jnp.sum(acc_ref[c * LANES:(c + 1) * LANES, :].T, axis=0, keepdims=True)
            for c in range(first, last)]
        return jnp.concatenate(sums, axis=0)

    def spread(x, ref, first):
        for c in range(x.shape[0]):
            at = (first + c) * LANES
            ref[at:at + LANES, :] = jnp.broadcast_to(x[c:c + 1, :], (LANES, LANES)).T

    def send_rows(it, h):
        mine = rowx.at[it, d, some_lines(h)]
        to_all("dp", d, nd, lambda j, axis: remote(mine, mine, ROW + 2 * it + h, **{axis: j}))

    def row_total(it, first, last):
        total = rowx[it, 0, first:last]
        for j in range(1, nd):
            total = total + rowx[it, j, first:last]
        return total

    def take_rows(it, h):
        wait_bytes(rsem.at[ROW + 2 * it + h], rowx.at[it, pl.ds(0, nd - 1), some_lines(h)])
        return 1.0 / (row_total(it, h * half_lines, (h + 1) * half_lines) * total_rows)

    def row_part(hb, hr):
        span = 64

        def step(i, carry):
            part = pl.ds(hr * half_rows + i * span, span)
            acc = None if hb == 0 else racc[part, :]
            for b in range(hb * half_blocks, (hb + 1) * half_blocks):
                for j in range(lane_chunks):
                    lanes = slice(j * LANES, (j + 1) * LANES)
                    term = e_ref[b, part, lanes] * v_ref[b, :, lanes]
                    acc = term if acc is None else acc + term
            racc[part, :] = acc
            return carry

        lax.fori_loop(0, half_rows // span, step, 0, unroll=True)

    def row_pass(it):
        take_cols(it, 0)
        row_part(0, 0)
        row_part(0, 1)
        take_cols(it, 1)
        for h in range(2):
            row_part(1, h)
            first, last = h * half_lines, (h + 1) * half_lines
            rowx[it, d, first:last] = dense(racc, first, last)
            send_rows(it, h)

    def col_part(it, hr, first, last):
        pair = 2

        def step(b2, carry):
            def inner(i, accs):
                accs = list(accs)
                for g in range(8):
                    part = pl.ds(hr * half_rows + i * 64 + g * 8, 8)
                    r = rb_ref[part, :]
                    for k in range(pair):
                        for j in range(lane_chunks):
                            n = k * lane_chunks + j
                            accs[n] = accs[n] + e_ref[b2 * pair + k, part, j * LANES:(j + 1) * LANES] * r
                return tuple(accs)

            spots = [(b2 * pair + k, slice(j * LANES, (j + 1) * LANES))
                     for k in range(pair) for j in range(lane_chunks)]
            if hr == 0:
                init = (jnp.zeros((8, LANES), F32),) * len(spots)
            else:
                init = tuple(cacc[b, :, lanes] for b, lanes in spots)
            accs = lax.fori_loop(0, half_rows // 64, inner, init, unroll=min(8, half_rows // 64))
            for acc, (b, lanes) in zip(accs, spots):
                if hr == 0:
                    cacc[b, :, lanes] = acc
                else:
                    colx[it, p, b, :, lanes] = jnp.sum(acc, axis=0, keepdims=True)
            return carry

        lax.fori_loop(first // pair, last // pair, step, 0)

    def col_pass(it):
        spread(take_rows(it - 1, 0), rb_ref, 0)
        col_part(it, 0, 0, np_)
        spread(take_rows(it - 1, 1), rb_ref, half_lines)
        for h in range(2):
            col_part(it, 1, h * half_blocks, (h + 1) * half_blocks)
            send_cols(it, h)

    def student_pass(first, last):
        def step(block, carry):
            for i in range(ntiles):
                part = slice(i * tile, (i + 1) * tile)
                dots = jnp.dot(s_all[part, :], w_all[block], preferred_element_type=F32)
                sums = fold_lanes(jnp.exp2(dots * as_ref[block]))
                sacc[part, :] += sums
            return carry
        lax.fori_loop(first, last, step, 0)

    send_cols(0, 0)
    send_cols(0, 1)
    sacc[...] = jnp.zeros_like(sacc)
    row_pass(0)
    col_pass(1)
    wait_bytes(rsem.at[S_GATHER], s_all.at[pl.ds(0, rows - chunk)])
    for c in range(lines):
        s_t[:, c * LANES:(c + 1) * LANES] = s_all[c * LANES:(c + 1) * LANES, :].T
    student_pass(0, 4)
    row_pass(1)
    student_pass(4, 8)
    soft[d] = dense(sacc, 0, lines)
    to_all("dp", d, nd, lambda j, axis: remote(soft.at[d], soft.at[d], SOFT, **{axis: j}))
    col_pass(2)
    wait_bytes(rsem.at[SOFT], soft.at[pl.ds(0, nd - 1)])
    soft_total = soft[0]
    for j in range(1, nd):
        soft_total = soft_total + soft[j]
    spread(1.0 / (soft_total * (total_rows * STUDENT_TEMP)), sb_ref, 0)
    lse = jnp.log(soft_total)
    row_pass(2)
    for h in range(2):
        spread(take_rows(2, h) * (1.0 / STUDENT_TEMP), rb_ref, h * half_lines)

    half_cols, quarter_cols = cols // 2, cols // 4

    def unit(block, side, g_tile, acc):
        base = side * half_cols
        columns = slice(base, base + half_cols)
        for i in range(ntiles):
            part = slice(i * tile, (i + 1) * tile)
            zb = jnp.dot(s_all[part, :], w_all[block, :, columns],
                         preferred_element_type=F32) * as_ref[block, :, columns]
            es = jnp.exp2(zb)
            q_scale = rb_ref[part, :]
            p_scale = sb_ref[part, :]
            for j in range(half_cols // LANES):
                lanes = slice(j * LANES, (j + 1) * LANES)
                here = slice(base + j * LANES, base + (j + 1) * LANES)
                q = e_ref[block, part, here] * v_ref[block, :, here] * q_scale
                g_tile[part, lanes] = (es[:, lanes] * p_scale - q).astype(BF16)
                acc = acc + fold_rows(q * zb[:, lanes])
        return acc

    owners = [opposite, plus, minus, p]
    z_copies = {}
    core_copies = {}

    def chip_sum(n, side):
        core_copies[n, side].wait_recv()
        if (n, side) == (1, 0):
            z_copies["a"].wait_recv()
            g_own[n, side] = g_own[n, side] + g_recv[n, side] + half_a[...]
        elif (n, side) == (2, 1):
            z_copies["b"].wait_recv()
            g_own[n, side] = g_own[n, side] + g_recv[n, side] + half_b[...]
        else:
            g_own[n, side] += g_recv[n, side]
        mine = g_own.at[n, side]
        if (n, side) == (0, 0):
            z_copies["a"] = go(remote(mine, half_a, G_HALF_A, proto=plus))
        elif (n, side) == (0, 1):
            z_copies["b"] = go(remote(mine, half_b, G_HALF_B, proto=minus))
        elif (n, side) == (1, 1):
            z_copies["plus"] = go(remote(mine, g_z.at[0, 1], G_PLUS, proto=plus))
        elif (n, side) == (2, 0):
            z_copies["minus"] = go(remote(mine, g_z.at[1, 0], G_MINUS, proto=minus))
        elif n != 3:
            send_last(side, 0)

    def send_last(side, quarter):
        lanes = pl.ds(quarter * quarter_cols, quarter_cols)
        to = plus if side == 0 else minus
        z_copies[side, quarter] = go(remote(
            g_own.at[side + 1, side, :, lanes], g_z.at[side, side, :, lanes],
            G_LAST + 2 * quarter + side, proto=to))

    def gradient(n, side, is_own, g_tile):
        dst = g_own if is_own else g_send
        dst[n, side] = jnp.dot(s_t[...], g_tile[...], preferred_element_type=F32)

    def send_core(n, side):
        core_copies[n, side] = go(remote(
            g_send.at[n, side], g_recv.at[n, side], G_CORE + 2 * n + side, proto=partner))

    order = [(0, 0), (0, 1), (1, 1), (2, 0), (3, 0), (3, 1), (1, 0), (2, 1)]
    units = [(n, side, is_own) for n, side in order for is_own in (False, True)]
    loss_acc = jnp.zeros((8, LANES), F32)
    waiting = None
    for k in range(len(units) + 2):
        if 2 < k <= len(units):
            gradient(*units[k - 1], g_tiles.at[(k - 1) % 2])
        if k < len(units):
            n, side, is_own = units[k]
            block = owners[n] if is_own else other(owners[n])
            loss_acc = unit(block, side, g_tiles.at[k % 2], loss_acc)
        if k < 2:
            gradient(*units[k], g_tiles.at[k % 2])
        if k == 0:
            send_core(*units[0][:2])
        elif k == 1:
            chip_sum(*units[1][:2])
        if waiting is not None:
            chip_sum(*waiting)
            waiting = None
        if 2 < k <= len(units):
            if units[k - 1][2]:
                waiting = units[k - 1][:2]
            else:
                send_core(*units[k - 1][:2])
    first_quarters = [z_copies[0, 0], z_copies[1, 0]]
    for side in (0, 1):
        send_last(side, 1)

    first_line = lax.broadcasted_iota(jnp.int32, (8, LANES), 0) == 0
    lse_sum = jnp.broadcast_to(jnp.sum(lse, axis=0, keepdims=True) * (1.0 / nd), (8, LANES))
    loss_scale = total_rows * STUDENT_TEMP / LOG2E
    loss_d[d] = jnp.where(first_line, lse_sum, 0.0) - loss_acc * loss_scale
    to_all("dp", d, nd, lambda j, axis: remote(
        loss_d.at[d], loss_d.at[d], LOSS_DP, **{axis: j}))
    wait_bytes(rsem.at[LOSS_DP], loss_d.at[pl.ds(0, nd - 1)])
    part = loss_d[0]
    for j in range(1, nd):
        part = part + loss_d[j]
    loss_p[p] = part
    to_all("proto", p, np_, lambda j, axis: remote(
        loss_p.at[p], loss_p.at[p], LOSS_PROTO, **{axis: j}))

    for quarter in (0, 1):
        lanes = slice(quarter * quarter_cols, (quarter + 1) * quarter_cols)
        for side in (0, 1):
            if quarter == 0:
                z_copies["minus" if side == 0 else "plus"].wait_recv()
            z_copies[side, quarter].wait_recv()
            n = 2 * quarter + side
            columns = slice(side * half_cols + lanes.start, side * half_cols + lanes.stop)
            grad = g_own[3, side, :, lanes] + g_z[0, side, :, lanes] + g_z[1, side, :, lanes]
            inv = inv_ref[p, :, columns]
            dirs = w_all[p, :, columns].astype(F32) * inv
            col = jnp.sum(dirs * grad, axis=0, keepdims=True)
            out_send[n] = (grad - dirs * col) * inv
            to_all("dp", d, nd, lambda j, axis: remote(
                out_send.at[n, pl.ds(j * own_depth, own_depth)], out_recv.at[n, d],
                OUT_A2A + n, **{axis: j}))
            out_recv[n, d] = out_send[n, own_rows]

    for n in range(4):
        wait_bytes(rsem.at[OUT_A2A + n], out_recv.at[n, pl.ds(0, nd - 1)])
        for j in range(nd):
            base = j * cols + (n % 2) * half_cols + (n // 2) * quarter_cols
            out[:, base:base + quarter_cols] = out_recv[n, j]

    wait_bytes(rsem.at[LOSS_PROTO], loss_p.at[pl.ds(0, np_ - 1)])
    whole = loss_p[0]
    for j in range(1, np_):
        whole = whole + loss_p[j]
    loss_out[0, 0] = jnp.sum(whole) * (1.0 / total_rows)

    for copy in copies:
        copy.wait_send()
    wait_bytes(ssem.at[W_A2A], w_all.at[0, pl.ds(0, depth - own_depth)])
    wait_bytes(ssem.at[T_GATHER], t_all.at[pl.ds(0, rows - chunk)])
    wait_bytes(ssem.at[S_GATHER], s_all.at[pl.ds(0, rows - chunk)])
    for it in range(ITERS):
        for h in range(2):
            wait_bytes(ssem.at[COL + 2 * it + h], colx.at[it, pl.ds(0, np_ - 1), some_blocks(h)])
            wait_bytes(ssem.at[ROW + 2 * it + h], rowx.at[it, pl.ds(0, nd - 1), some_lines(h)])
    wait_bytes(ssem.at[SOFT], soft.at[pl.ds(0, nd - 1)])
    for n in range(4):
        wait_bytes(ssem.at[OUT_A2A + n], out_recv.at[n, pl.ds(0, nd - 1)])
    wait_bytes(ssem.at[LOSS_PROTO], loss_p.at[pl.ds(0, np_ - 1)])
    wait_bytes(ssem.at[LOSS_DP], loss_d.at[pl.ds(0, nd - 1)])


def body(nd, np_, teacher_feat, student_feat, proto_weight):
    block_rows, depth = teacher_feat.shape
    own_depth, block_cols = proto_weight.shape
    chunk, cols = block_rows // np_, block_cols // nd
    rows = chunk * nd
    tile = min(256, rows)
    vmem = pltpu.VMEM
    out, loss = pl.pallas_call(
        functools.partial(kernel, nd, np_, tile),
        out_shape=(
            jax.ShapeDtypeStruct((own_depth, block_cols), F32),
            jax.ShapeDtypeStruct((1, 1), F32),
        ),
        in_specs=[pl.BlockSpec(memory_space=pl.ANY)] * 3,
        out_specs=[pl.BlockSpec(memory_space=vmem), pl.BlockSpec(memory_space=pltpu.SMEM)],
        scratch_shapes=[
            vmem((chunk, depth), BF16),
            vmem((chunk, depth), BF16),
            vmem((own_depth, block_cols), BF16),
            vmem((rows, depth), BF16),
            vmem((rows, depth), BF16),
            vmem((depth, rows), BF16),
            vmem((np_, depth, cols), BF16),
            vmem((np_, rows, cols), F32),
            vmem((np_, 1, cols), F32),
            vmem((np_, 1, cols), F32),
            vmem((np_, 1, cols), F32),
            vmem((np_, 1, cols), F32),
            vmem((rows, LANES), F32),
            vmem((rows, LANES), F32),
            vmem((rows, LANES), F32),
            vmem((rows, LANES), F32),
            vmem((np_, 8, cols), F32),
            vmem((ITERS, np_, np_, 1, cols), F32),
            vmem((ITERS, nd, rows // LANES, LANES), F32),
            vmem((nd, rows // LANES, LANES), F32),
            vmem((2, rows, cols // 2), BF16),
            vmem((4, 2, depth, cols // 2), F32),
            vmem((4, 2, depth, cols // 2), F32),
            vmem((4, 2, depth, cols // 2), F32),
            vmem((depth, cols // 2), F32),
            vmem((depth, cols // 2), F32),
            vmem((2, 2, depth, cols // 2), F32),
            vmem((4, depth, cols // 4), F32),
            vmem((4, nd, own_depth, cols // 4), F32),
            vmem((np_, 8, LANES), F32),
            vmem((nd, 8, LANES), F32),
            pltpu.SemaphoreType.DMA((STAGES,)),
            pltpu.SemaphoreType.DMA((STAGES,)),
            pltpu.SemaphoreType.DMA((4,)),
        ],
        compiler_params=pltpu.CompilerParams(
            collective_id=0, has_side_effects=True, vmem_limit_bytes=62 * 1024 * 1024),
        cost_estimate=pl.CostEstimate(
            flops=6 * rows * cols * np_ * depth, bytes_accessed=2 ** 21,
            transcendentals=2 * rows * cols * np_),
    )(teacher_feat, student_feat, proto_weight)
    return out, jnp.reshape(loss, ())


def solution(mesh):
    nd, np_ = mesh.shape["dp"], mesh.shape["proto"]
    in_specs = (P("dp", None), P("dp", None), P("dp", "proto"))
    out_specs = (P("dp", "proto"), P())
    return jax.shard_map(
        functools.partial(body, nd, np_), mesh=mesh, in_specs=in_specs, out_specs=out_specs, check_vma=False)
```
